32 devices in a mesh: shots: 2 (over y), lat: 16 (over z, x, core).
Axes of the slice: x: 2, y: 2, z: 4, core: 2. Of those that a mesh axis runs over, the one named last changes fastest.
Arguments:
- source_field: float32 [2, 2, 2048, 2048], P(None, 'shots', 'lat'), parts along dimension 1, may hold values from -6 to 6
- rec_blocks: float32 [512, 2, 1, 128], P(('shots', 'lat')), parts along dimension 0, may hold values from -6 to 6
- dest_device: int32 [512, 1], P(('shots', 'lat')), parts along dimension 0, may hold values from 0 to 15; in each aligned block of 16 rows (0 to 15, 16 to 31, ...) at most 2 rows name the same one
- dest_bin: int32 [512], P(('shots', 'lat')), parts along dimension 0, may hold values from 0 to 2047
- slowness: float32 [1, 2048, 2048], P(None, 'lat'), may hold values from 0.25 to 0.7
- ref_index: int32 [1, 2048, 2048], P(None, 'lat'), may hold values from 0 to 1
- ref_slow: float32 [1, 2], replicated, may hold values from 0.25 to 0.7
- omega: float32 [1], replicated, may hold values from 190 to 380
Outputs:
- image: float32 [2, 2048, 2048], P('shots', 'lat'), parts along dimension 0
The draws below stay inside these ranges and needn't reach their ends.
There are 2 independent parts, one for each index of `shots`. The reference program is written for one: setup_inputs(seed, part) draws one part's arguments, and reference() takes and returns one part's arrays. A program takes and returns all parts, laid end to end along the dimension named above; an argument that names none is the same for every part. Nothing has to cross between parts.
Inputs may be any that keep to these rules, and one draw needn't show every extreme that they name: `dest_device`: among the trace blocks of one device no destination device is named more than 2 times, a bound that some block reaches.
All inputs are finite; a program needn't handle non-finite values.
Results may differ from the reference program's by a relative error of at most 0.0003.
Values sent between devices are 32-bit elements; how exact they have to be, the bound alone decides.
A program may use at most 64 MiB of HBM per device.

```python
import math
import jax
import jax.numpy as jnp
import numpy as np
from jax import lax

NX = 2048
NY = 2048
NF = 1
NZ = 1
NREF = 2
BW = 128
CAP = 2
BINS = 2048
BLK_DEV = 16
BLOCKS = 256
N_LAT = 16


def draw_source_field(key, part):
    jitter_key, scale_key = jax.random.split(jax.random.fold_in(key, 7))
    row_index = jnp.arange(NX, dtype=jnp.int32)
    col_index = jnp.arange(NY, dtype=jnp.int32)
    parity = ((row_index[:, None] + col_index[None, :]) % 2).astype(jnp.float32)
    checker = 1.0 - 2.0 * parity
    row_wave = jnp.cos(2.0 * math.pi * row_index.astype(jnp.float32) / NX)
    col_wave = jnp.cos(2.0 * math.pi * col_index.astype(jnp.float32) / NY)
    envelope = 0.75 + 0.25 * row_wave[:, None] * col_wave[None, :]
    pattern = checker * envelope
    component = jnp.array([1.0, -0.6], dtype=jnp.float32)
    freq_scale = jax.random.uniform(scale_key, (2, NF), jnp.float32, 0.8, 1.0)
    strength = 3.0
    jitter = jnp.clip(jax.random.normal(jitter_key, (2, NF, NX, NY), jnp.float32), -3.0, 3.0)
    levels = strength * component[:, None] * freq_scale
    return levels[:, :, None, None] * pattern[None, None] + jitter


def place_ends(entries, key, smallest, top_value):
    dims = entries.shape
    spot = [jax.random.randint(jax.random.fold_in(key, axis), (), 0, dims[axis]) for axis in range(len(dims))]
    entries = entries.at[tuple(spot)].set(smallest)
    longest = dims.index(max(dims))
    spot[longest] = (spot[longest] + 1) % dims[longest]
    return entries.at[tuple(spot)].set(top_value)


def shard_levels(key, shape, shards, smallest, high):
    level, own = 1.0, jax.random.fold_in(key, 6)
    for dim, parts in shards:
        steps = jnp.exp(jax.random.uniform(jax.random.fold_in(own, dim), (parts,), jnp.float32, smallest / len(shards), high / len(shards)))
        level = level * jnp.repeat(steps, shape[dim] // parts).reshape([-1 if axis == dim else 1 for axis in range(len(shape))])
    return level


def assign_block(rng, own, number, rows, amount, top, bound, skew):
    order = jax.random.permutation(rng, amount)
    heavy_load, ordinary = shares(amount, rows * top, bound, skew, True), shares(amount, rows * top, bound, skew, False)
    places = jnp.arange(amount)

    def named(lengths, rotation):
        used = int((lengths > 0).sum())
        fixed = max(1, used // 4)
        shifted = fixed + (places - fixed + rotation * (used - fixed)) % max(1, amount - fixed)
        return jnp.zeros((amount,), jnp.int32).at[order[jnp.where(places < fixed, places, shifted)]].set(jnp.asarray(lengths, jnp.int32))

    lengths = jnp.where(number % 4 == 0, named(heavy_load, number // 4), named(ordinary, number - number // 4 - 1))
    mixed = jax.random.permutation(jax.random.fold_in(own, 3), amount)
    source_of, sink = mixed[0:amount // 2 * 2:2], mixed[1:amount // 2 * 2:2]
    margin = jnp.minimum(lengths[source_of] - 1, bound - lengths[sink]) // 2
    margin = jnp.where((source_of == order[0]) | (sink == order[0]) | (lengths[sink] == 0), 0, jnp.maximum(margin, 0))
    shifted = jax.random.randint(jax.random.fold_in(own, 4), (amount // 2,), 0, 1 << 20) % (margin + 1)
    lengths = lengths.at[source_of].add(-shifted).at[sink].add(shifted)
    labels = jnp.searchsorted(jnp.cumsum(lengths), jnp.arange(rows * top), side="right").astype(jnp.int32)
    table = labels.reshape(top, rows).T
    table = table[jax.random.permutation(jax.random.fold_in(own, 1), rows)]
    rotation = jax.random.randint(jax.random.fold_in(own, 2), (rows, 1), 0, top)
    return jnp.take_along_axis(table, (jnp.arange(top)[None, :] + rotation) % top, axis=1)


def shares(number_of, total, limit, skew, full):
    weights = [(1 << 20) // math.isqrt(standing ** skew) + 1 for standing in range(1, number_of + 1)]
    largest = limit if full else min(limit, max(-(-total // number_of), total * weights[0] // sum(weights)))
    least = 1 if total - largest >= number_of - 1 else 0
    holding, rest = [largest] + [least] * (number_of - 1), total - largest - least * (number_of - 1)
    while rest > 0:
        candidates = [i for i in range(1, number_of) if holding[i] < largest] or [i for i in range(1, number_of) if holding[i] < limit]
        pool, left = sum([weights[i] for i in candidates]), rest
        for i in candidates:
            extra = min(limit - holding[i], max(1, left * weights[i] // pool), rest)
            holding[i] = holding[i] + extra
            rest = rest - extra
    return np.array(holding)


def noise(stream_key, shape, spread, bound, shards=(), kind=jnp.bfloat16):
    drawn = spread * jax.random.normal(stream_key, shape, jnp.float32)
    if shards:
        drawn = drawn * shard_levels(stream_key, shape, shards, -0.22, 0.18)
    return jnp.clip(drawn, -bound, bound).astype(kind)


def setup_inputs(seed: int = 0, part: int = 0) -> dict:
    key_list = jax.random.split(jax.random.key(seed), 9)
    part_keys = jax.random.split(jax.random.fold_in(key_list[8], part), 9)
    source_field = draw_source_field(jax.random.fold_in(jax.random.fold_in(key_list[8], part), 71), part)
    rec_blocks = noise(part_keys[1], (BLOCKS, 2, NF, BW), 1.0, 6.0, ((0, 16),), jnp.float32)
    dest_device_keys = jax.random.split(jax.random.fold_in(part_keys[2], 1), BLOCKS // BLK_DEV)
    dest_device_turns = jax.random.permutation(jax.random.fold_in(part_keys[2], 3), BLOCKS // BLK_DEV)
    dest_device = jax.vmap(lambda own, number: assign_block(jax.random.fold_in(part_keys[2], 2), own, number, BLK_DEV, N_LAT, 1, CAP, 2))(dest_device_keys, dest_device_turns).reshape((BLOCKS, 1))
    dest_bin = place_ends(jax.random.randint(part_keys[3], (BLOCKS,), 0, BINS), jax.random.fold_in(part_keys[3], 1), 0, BINS - 1).astype(jnp.int32)
    slowness = jnp.clip(jnp.exp(math.log(0.7) - 1.0296194 * jax.random.uniform(key_list[4], (NZ, NX, NY), jnp.float32) ** shard_levels(key_list[4], (NZ, NX, NY), ((1, 16),), -0.2, 0.2)), 0.25, 0.7)
    ref_index = place_ends(jax.random.randint(key_list[5], (NZ, NX, NY), 0, NREF), jax.random.fold_in(key_list[5], 1), 0, NREF - 1).astype(jnp.int32)
    ref_slow = jnp.clip(jax.random.uniform(key_list[6], (NZ, NREF), jnp.float32, 0.25, 0.7), 0.25, 0.7)
    omega = jnp.clip(jax.random.uniform(key_list[7], (NF,), jnp.float32, 190.0, 380.0), 190.0, 380.0)
    return {"source_field": source_field, "rec_blocks": rec_blocks, "dest_device": dest_device, "dest_bin": dest_bin, "slowness": slowness, "ref_index": ref_index, "ref_slow": ref_slow, "omega": omega}


def wave_numbers(length):
    index = jnp.arange(length, dtype=jnp.int32)
    signed = jnp.where(index < length // 2, index, index - length)
    return signed.astype(jnp.float32) * (2.0 * math.pi / (length * 0.01))

def reference(source_field, rec_blocks, dest_device, dest_bin, slowness, ref_index, ref_slow, omega):
    flat = rec_blocks.reshape(BLOCKS, 2 * NF * BW)
    target = (dest_device[:, 0] * BINS + dest_bin).astype(jnp.int32)
    binned = jax.ops.segment_sum(flat, target, num_segments=NX * (NY // BW))
    binned = binned.reshape(NX, NY // BW, 2, NF, BW).transpose(2, 3, 0, 1, 4).reshape(2, NF, NX, NY)
    field_real = jnp.concatenate([source_field[0], binned[0]], axis=0)
    field_imag = jnp.concatenate([source_field[1], binned[1]], axis=0)
    signed = jnp.concatenate([-omega, omega])
    sense = jnp.sign(signed)[:, None, None]
    radial = wave_numbers(NX)[:, None] ** 2 + wave_numbers(NY)[None, :] ** 2
    images = []
    for depth_index in range(NZ):
        spectrum = jnp.fft.fft2(lax.complex(field_real, field_imag))
        new_real = jnp.zeros_like(field_real)
        new_imag = jnp.zeros_like(field_imag)
        for which in range(NREF):
            speed = ref_slow[depth_index, which]
            argument = (signed ** 2)[:, None, None] * speed ** 2 - radial[None]
            amplitude = jnp.exp(-jnp.sqrt(jnp.maximum(-argument, 0.0)) * 0.01)
            phase = sense * jnp.sqrt(jnp.maximum(argument, 0.0)) * 0.01
            shifter = lax.complex(amplitude * jnp.cos(phase), amplitude * jnp.sin(phase))
            spatial = jnp.fft.ifft2(spectrum * shifter)
            angle = signed[:, None, None] * (slowness[depth_index] - speed)[None] * 0.01
            corrected = spatial * lax.complex(jnp.cos(angle), jnp.sin(angle))
            chosen = (ref_index[depth_index] == which)[None]
            new_real = jnp.where(chosen, jnp.real(corrected), new_real)
            new_imag = jnp.where(chosen, jnp.imag(corrected), new_imag)
        field_real, field_imag = (new_real, new_imag)
        images.append(lax.optimization_barrier(jnp.sum(field_real[:NF] * field_real[NF:] + field_imag[:NF] * field_imag[NF:], axis=0)))
    return jnp.stack(images)
```

```python
from functools import partial
import math

import jax
import jax.numpy as jnp
from jax import lax
from jax.sharding import PartitionSpec as P

NREF = 2
CAP = 2


SPACING = 0.01
DEPTH_STEP = 0.01
RADIX = 128


def angle_table(size, direction):
    index = jnp.arange(size, dtype=jnp.int32)
    product = index[:, None] * index[None, :] % size
    angle = direction * 2.0 * math.pi * product.astype(jnp.float32) / size
    return (jnp.cos(angle), jnp.sin(angle))


def twist_table(length, direction):
    outer_index = jnp.arange(length // RADIX, dtype=jnp.int32)
    radix_index = jnp.arange(RADIX, dtype=jnp.int32)
    product = outer_index[:, None] * radix_index[None, :] % length
    angle = direction * 2.0 * math.pi * product.astype(jnp.float32) / length
    return (jnp.cos(angle), jnp.sin(angle))


def complex_einsum(formula, real_in, imag_in, real_mat, imag_mat):
    multiply = partial(jnp.einsum, formula, precision=lax.Precision.HIGHEST)
    return (
        multiply(real_in, real_mat) - multiply(imag_in, imag_mat),
        multiply(real_in, imag_mat) + multiply(imag_in, real_mat),
    )


def transform(real_in, imag_in, trailing, direction):
    length = real_in.shape[-2] if trailing else real_in.shape[-1]
    inner = length // RADIX
    first_real, first_imag = angle_table(inner, direction)
    second_real, second_imag = angle_table(RADIX, direction)
    twist_real, twist_imag = twist_table(length, direction)
    initial = real_in.shape
    if trailing:
        shape = initial[:-2] + (inner, RADIX, initial[-1])
        twist_real = twist_real[:, :, None]
        twist_imag = twist_imag[:, :, None]
        tail = "z"
    else:
        shape = initial[:-1] + (inner, RADIX)
        tail = ""
    work_real = real_in.reshape(shape)
    work_imag = imag_in.reshape(shape)
    if direction < 0:
        work_real, work_imag = complex_einsum(
            "...ab" + tail + ",ac->...cb" + tail, work_real, work_imag, first_real, first_imag
        )
        work_real, work_imag = (
            work_real * twist_real - work_imag * twist_imag,
            work_real * twist_imag + work_imag * twist_real,
        )
        work_real, work_imag = complex_einsum(
            "...cb" + tail + ",bd->...cd" + tail, work_real, work_imag, second_real, second_imag
        )
    else:
        work_real, work_imag = complex_einsum(
            "...cb" + tail + ",bd->...cd" + tail, work_real, work_imag, second_real, second_imag
        )
        work_real, work_imag = (
            work_real * twist_real - work_imag * twist_imag,
            work_real * twist_imag + work_imag * twist_real,
        )
        work_real, work_imag = complex_einsum(
            "...cb" + tail + ",ca->...ab" + tail, work_real, work_imag, first_real, first_imag
        )
        work_real = work_real / length
        work_imag = work_imag / length
    return (work_real.reshape(initial), work_imag.reshape(initial))


def permuted_numbers(positions, length):
    inner = length // RADIX
    index = positions // RADIX + inner * (positions % RADIX)
    signed = jnp.where(index < length // 2, index, index - length)
    return signed.astype(jnp.float32) * (2.0 * math.pi / (length * SPACING))


def per_device(
    source_field, rec_blocks, dest_device, dest_bin, slowness, ref_index, ref_slow, omega
):
    lanes = lax.axis_size("lat")
    count_blocks = rec_blocks.shape[0]
    freqs = rec_blocks.shape[2]
    block_width = rec_blocks.shape[3]
    rows_here = source_field.shape[2]
    columns = source_field.shape[3]
    bins_here = rows_here * (columns // block_width)
    slots = lanes * CAP
    flat = rec_blocks.reshape(count_blocks, 2 * freqs * block_width)
    onehot = (dest_device == jnp.arange(lanes, dtype=jnp.int32)[None, :]).astype(jnp.int32)
    order = jnp.arange(count_blocks, dtype=jnp.int32)
    before = (order[None, :] < order[:, None]).astype(jnp.int32)
    earlier = jnp.sum(before[:, :, None] * onehot[None, :, :], axis=1)
    ranking = jnp.sum(onehot * earlier, axis=1)
    slot_of = dest_device[:, 0] * CAP + ranking
    placing = slot_of[None, :] == jnp.arange(slots, dtype=jnp.int32)[:, None]
    outgoing = jnp.dot(placing.astype(jnp.float32), flat, precision=lax.Precision.HIGHEST)
    labels = jnp.sum(jnp.where(placing, (dest_bin + 1)[None, :], 0), axis=1).astype(jnp.float32)
    arrived, arrived_labels = (
        lax.all_to_all(
            outgoing.reshape(lanes, CAP, -1), "lat", split_axis=0, concat_axis=0, tiled=True
        ),
        lax.all_to_all(labels.reshape(lanes, CAP), "lat", split_axis=0, concat_axis=0, tiled=True),
    )
    bin_labels = arrived_labels.reshape(slots).astype(jnp.int32) - 1
    gathering = (bin_labels[None, :] == jnp.arange(bins_here, dtype=jnp.int32)[:, None]).astype(
        jnp.float32
    )
    binned = jnp.dot(gathering, arrived.reshape(slots, -1), precision=lax.Precision.HIGHEST)
    binned = binned.reshape(rows_here, columns // block_width, 2, freqs, block_width)
    received = binned.transpose(2, 3, 0, 1, 4).reshape(2, freqs, rows_here, columns)
    field_real = jnp.concatenate([source_field[0], received[0]], axis=0)
    field_imag = jnp.concatenate([source_field[1], received[1]], axis=0)
    signed = jnp.concatenate([-omega, omega])
    spec_real, spec_imag = transform(field_real, field_imag, False, -1.0)
    carried = jnp.broadcast_to(signed[:, None, None], (2 * freqs, 1, lanes))
    part_real = lax.all_to_all(spec_real, "lat", split_axis=2, concat_axis=1, tiled=True)
    part_imag = lax.all_to_all(spec_imag, "lat", split_axis=2, concat_axis=1, tiled=True)
    part_params = lax.all_to_all(carried, "lat", split_axis=2, concat_axis=1, tiled=True)
    total_rows = part_real.shape[1]
    local_cols = part_real.shape[2]
    freq_real, freq_imag = transform(part_real, part_imag, True, -1.0)
    kx_values = permuted_numbers(jnp.arange(total_rows, dtype=jnp.int32), total_rows)
    positions = lax.axis_index("lat") * local_cols + jnp.arange(local_cols, dtype=jnp.int32)
    ky_values = permuted_numbers(positions, lanes * local_cols)
    radial = kx_values[:, None] ** 2 + ky_values[None, :] ** 2
    freq_signed = part_params[:, 0, 0]
    sense = jnp.sign(freq_signed)[:, None, None]
    shifted_real = []
    shifted_imag = []
    for propagate_which in range(NREF):
        propagate_speed = ref_slow[0, propagate_which]
        argument = (freq_signed**2)[:, None, None] * propagate_speed**2 - radial[None]
        amplitude = jnp.exp(-jnp.sqrt(jnp.maximum(-argument, 0.0)) * DEPTH_STEP)
        phase = sense * jnp.sqrt(jnp.maximum(argument, 0.0)) * DEPTH_STEP
        factor_real = amplitude * jnp.cos(phase)
        factor_imag = amplitude * jnp.sin(phase)
        moved_real = freq_real * factor_real - freq_imag * factor_imag
        moved_imag = freq_real * factor_imag + freq_imag * factor_real
        moved_real, moved_imag = transform(moved_real, moved_imag, True, 1.0)
        shifted_real.append(moved_real)
        shifted_imag.append(moved_imag)
    stacked_real = jnp.stack(shifted_real, axis=1)
    stacked_imag = jnp.stack(shifted_imag, axis=1)
    back_real = lax.all_to_all(stacked_real, "lat", split_axis=2, concat_axis=3, tiled=True)
    back_imag = lax.all_to_all(stacked_imag, "lat", split_axis=2, concat_axis=3, tiled=True)
    space_real, space_imag = transform(back_real, back_imag, False, 1.0)
    new_real = jnp.zeros_like(field_real)
    new_imag = jnp.zeros_like(field_imag)
    for which in range(NREF):
        speed = ref_slow[0, which]
        angle = signed[:, None, None] * (slowness[0] - speed)[None] * DEPTH_STEP
        cosine = jnp.cos(angle)
        sine = jnp.sin(angle)
        fixed_real = space_real[:, which] * cosine - space_imag[:, which] * sine
        fixed_imag = space_real[:, which] * sine + space_imag[:, which] * cosine
        chosen = (ref_index[0] == which)[None]
        new_real = jnp.where(chosen, fixed_real, new_real)
        new_imag = jnp.where(chosen, fixed_imag, new_imag)
    images = [
        jnp.sum(new_real[:freqs] * new_real[freqs:] + new_imag[:freqs] * new_imag[freqs:], axis=0)
    ]
    return jnp.stack(images)


def solution(mesh):
    return jax.shard_map(
        per_device,
        mesh=mesh,
        in_specs=(
            P(None, "shots", "lat", None),
            P(("shots", "lat"), None, None, None),
            P(("shots", "lat"), None),
            P(("shots", "lat")),
            P(None, "lat", None),
            P(None, "lat", None),
            P(),
            P(),
        ),
        out_specs=P("shots", "lat", None),
        check_vma=False,
    )
```

```python
from functools import partial
import math

import jax
import jax.numpy as jnp
import numpy as np
from jax import lax
from jax.experimental import pallas as pl
from jax.experimental.pallas import tpu as pltpu
from jax.sharding import PartitionSpec as P

NREF = 2
CAP = 2


SPACING = 0.01
DEPTH_STEP = 0.01
RADIX = 128


def angle_table(size, direction):
    index = jnp.arange(size, dtype=jnp.int32)
    product = index[:, None] * index[None, :] % size
    angle = direction * 2.0 * math.pi * product.astype(jnp.float32) / size
    return (jnp.cos(angle), jnp.sin(angle))


def twist_table(length, direction):
    outer_index = jnp.arange(length // RADIX, dtype=jnp.int32)
    radix_index = jnp.arange(RADIX, dtype=jnp.int32)
    product = outer_index[:, None] * radix_index[None, :] % length
    angle = direction * 2.0 * math.pi * product.astype(jnp.float32) / length
    return (jnp.cos(angle), jnp.sin(angle))


def complex_einsum(formula, real_in, imag_in, real_mat, imag_mat):
    multiply = partial(jnp.einsum, formula, precision=lax.Precision.HIGHEST)
    return (
        multiply(real_in, real_mat) - multiply(imag_in, imag_mat),
        multiply(real_in, imag_mat) + multiply(imag_in, real_mat),
    )


def transform(real_in, imag_in, trailing, direction):
    length = real_in.shape[-2] if trailing else real_in.shape[-1]
    inner = length // RADIX
    first_real, first_imag = angle_table(inner, direction)
    second_real, second_imag = angle_table(RADIX, direction)
    twist_real, twist_imag = twist_table(length, direction)
    initial = real_in.shape
    if trailing:
        shape = initial[:-2] + (inner, RADIX, initial[-1])
        twist_real = twist_real[:, :, None]
        twist_imag = twist_imag[:, :, None]
        tail = "z"
    else:
        shape = initial[:-1] + (inner, RADIX)
        tail = ""
    work_real = real_in.reshape(shape)
    work_imag = imag_in.reshape(shape)
    if direction < 0:
        work_real, work_imag = complex_einsum(
            "...ab" + tail + ",ac->...cb" + tail, work_real, work_imag, first_real, first_imag
        )
        work_real, work_imag = (
            work_real * twist_real - work_imag * twist_imag,
            work_real * twist_imag + work_imag * twist_real,
        )
        work_real, work_imag = complex_einsum(
            "...cb" + tail + ",bd->...cd" + tail, work_real, work_imag, second_real, second_imag
        )
    else:
        work_real, work_imag = complex_einsum(
            "...cb" + tail + ",bd->...cd" + tail, work_real, work_imag, second_real, second_imag
        )
        work_real, work_imag = (
            work_real * twist_real - work_imag * twist_imag,
            work_real * twist_imag + work_imag * twist_real,
        )
        work_real, work_imag = complex_einsum(
            "...cb" + tail + ",ca->...ab" + tail, work_real, work_imag, first_real, first_imag
        )
        work_real = work_real / length
        work_imag = work_imag / length
    return (work_real.reshape(initial), work_imag.reshape(initial))


def permuted_numbers(positions, length):
    inner = length // RADIX
    index = positions // RADIX + inner * (positions % RADIX)
    signed = jnp.where(index < length // 2, index, index - length)
    return signed.astype(jnp.float32) * (2.0 * math.pi / (length * SPACING))


def general(
    source_field, rec_blocks, dest_device, dest_bin, slowness, ref_index, ref_slow, omega
):
    lanes = lax.axis_size("lat")
    count_blocks = rec_blocks.shape[0]
    freqs = rec_blocks.shape[2]
    block_width = rec_blocks.shape[3]
    rows_here = source_field.shape[2]
    columns = source_field.shape[3]
    bins_here = rows_here * (columns // block_width)
    slots = lanes * CAP
    flat = rec_blocks.reshape(count_blocks, 2 * freqs * block_width)
    onehot = (dest_device == jnp.arange(lanes, dtype=jnp.int32)[None, :]).astype(jnp.int32)
    order = jnp.arange(count_blocks, dtype=jnp.int32)
    before = (order[None, :] < order[:, None]).astype(jnp.int32)
    earlier = jnp.sum(before[:, :, None] * onehot[None, :, :], axis=1)
    ranking = jnp.sum(onehot * earlier, axis=1)
    slot_of = dest_device[:, 0] * CAP + ranking
    placing = slot_of[None, :] == jnp.arange(slots, dtype=jnp.int32)[:, None]
    outgoing = jnp.dot(placing.astype(jnp.float32), flat, precision=lax.Precision.HIGHEST)
    labels = jnp.sum(jnp.where(placing, (dest_bin + 1)[None, :], 0), axis=1).astype(jnp.float32)
    arrived, arrived_labels = (
        lax.all_to_all(
            outgoing.reshape(lanes, CAP, -1), "lat", split_axis=0, concat_axis=0, tiled=True
        ),
        lax.all_to_all(labels.reshape(lanes, CAP), "lat", split_axis=0, concat_axis=0, tiled=True),
    )
    bin_labels = arrived_labels.reshape(slots).astype(jnp.int32) - 1
    gathering = (bin_labels[None, :] == jnp.arange(bins_here, dtype=jnp.int32)[:, None]).astype(
        jnp.float32
    )
    binned = jnp.dot(gathering, arrived.reshape(slots, -1), precision=lax.Precision.HIGHEST)
    binned = binned.reshape(rows_here, columns // block_width, 2, freqs, block_width)
    received = binned.transpose(2, 3, 0, 1, 4).reshape(2, freqs, rows_here, columns)
    field_real = jnp.concatenate([source_field[0], received[0]], axis=0)
    field_imag = jnp.concatenate([source_field[1], received[1]], axis=0)
    signed = jnp.concatenate([-omega, omega])
    spec_real, spec_imag = transform(field_real, field_imag, False, -1.0)
    carried = jnp.broadcast_to(signed[:, None, None], (2 * freqs, 1, lanes))
    part_real = lax.all_to_all(spec_real, "lat", split_axis=2, concat_axis=1, tiled=True)
    part_imag = lax.all_to_all(spec_imag, "lat", split_axis=2, concat_axis=1, tiled=True)
    part_params = lax.all_to_all(carried, "lat", split_axis=2, concat_axis=1, tiled=True)
    total_rows = part_real.shape[1]
    local_cols = part_real.shape[2]
    freq_real, freq_imag = transform(part_real, part_imag, True, -1.0)
    kx_values = permuted_numbers(jnp.arange(total_rows, dtype=jnp.int32), total_rows)
    positions = lax.axis_index("lat") * local_cols + jnp.arange(local_cols, dtype=jnp.int32)
    ky_values = permuted_numbers(positions, lanes * local_cols)
    radial = kx_values[:, None] ** 2 + ky_values[None, :] ** 2
    freq_signed = part_params[:, 0, 0]
    sense = jnp.sign(freq_signed)[:, None, None]
    shifted_real = []
    shifted_imag = []
    for propagate_which in range(NREF):
        propagate_speed = ref_slow[0, propagate_which]
        argument = (freq_signed**2)[:, None, None] * propagate_speed**2 - radial[None]
        amplitude = jnp.exp(-jnp.sqrt(jnp.maximum(-argument, 0.0)) * DEPTH_STEP)
        phase = sense * jnp.sqrt(jnp.maximum(argument, 0.0)) * DEPTH_STEP
        factor_real = amplitude * jnp.cos(phase)
        factor_imag = amplitude * jnp.sin(phase)
        moved_real = freq_real * factor_real - freq_imag * factor_imag
        moved_imag = freq_real * factor_imag + freq_imag * factor_real
        moved_real, moved_imag = transform(moved_real, moved_imag, True, 1.0)
        shifted_real.append(moved_real)
        shifted_imag.append(moved_imag)
    stacked_real = jnp.stack(shifted_real, axis=1)
    stacked_imag = jnp.stack(shifted_imag, axis=1)
    back_real = lax.all_to_all(stacked_real, "lat", split_axis=2, concat_axis=3, tiled=True)
    back_imag = lax.all_to_all(stacked_imag, "lat", split_axis=2, concat_axis=3, tiled=True)
    space_real, space_imag = transform(back_real, back_imag, False, 1.0)
    new_real = jnp.zeros_like(field_real)
    new_imag = jnp.zeros_like(field_imag)
    for which in range(NREF):
        speed = ref_slow[0, which]
        angle = signed[:, None, None] * (slowness[0] - speed)[None] * DEPTH_STEP
        cosine = jnp.cos(angle)
        sine = jnp.sin(angle)
        fixed_real = space_real[:, which] * cosine - space_imag[:, which] * sine
        fixed_imag = space_real[:, which] * sine + space_imag[:, which] * cosine
        chosen = (ref_index[0] == which)[None]
        new_real = jnp.where(chosen, fixed_real, new_real)
        new_imag = jnp.where(chosen, fixed_imag, new_imag)
    images = [
        jnp.sum(new_real[:freqs] * new_real[freqs:] + new_imag[:freqs] * new_imag[freqs:], axis=0)
    ]
    return jnp.stack(images)


INNER = 16
LENGTH = INNER * RADIX
PARAMS = pltpu.CompilerParams(vmem_limit_bytes=50 * 2**20)


def dft_tables(direction, left, scale):
    index = np.arange(RADIX)
    angle = direction * 2.0 * np.pi * (index[:, None] * index[None, :] % RADIX) / RADIX
    cosine, sine = np.cos(angle) * scale, np.sin(angle) * scale
    whole = np.block([[cosine, -sine], [sine, cosine]] if left else [[cosine, sine], [-sine, cosine]])
    whole = jnp.asarray(whole.astype(np.float32))
    high = whole.astype(jnp.bfloat16)
    low = (whole - high.astype(jnp.float32)).astype(jnp.bfloat16)
    return jnp.stack([high, low])


def twiddles(direction):
    angle = direction * 2.0 * np.pi * (np.arange(INNER)[:, None] * np.arange(RADIX)[None, :]) / LENGTH
    return np.stack([np.cos(angle), np.sin(angle)]).astype(np.float32)


def butterflies(values, direction):
    count = len(values)
    if count == 1:
        return values
    even = butterflies(values[0::2], direction)
    odd = butterflies(values[1::2], direction)
    first, second = [], []
    for k in range(count // 2):
        (er, ei), (pr, pi) = even[k], odd[k]
        if k == 0:
            tr, ti = pr, pi
        elif 4 * k == count:
            tr, ti = (-pi, pr) if direction > 0 else (pi, -pr)
        else:
            c = math.cos(2.0 * math.pi * k / count)
            d = direction * math.sin(2.0 * math.pi * k / count)
            tr, ti = pr * c - pi * d, pr * d + pi * c
        first.append((er + tr, ei + ti))
        second.append((er - tr, ei - ti))
    return first + second


def halves(value):
    high = value.astype(jnp.bfloat16)
    return high, (value - high.astype(jnp.float32)).astype(jnp.bfloat16)


def mul(a, b):
    return jnp.dot(a, b, preferred_element_type=jnp.float32)


def right_product(value, table):
    high, low = halves(value)
    return mul(low, table[0]) + mul(high, table[1]) + mul(high, table[0])


def left_product(table, value):
    high, low = halves(value)
    return mul(table[1], high) + mul(table[0], low) + mul(table[0], high)


def row_chunk(i):
    return pl.ds(pl.multiple_of(i * 8, 8), 8)


def forward_columns(field, table, twist, out, work):
    rows = field.shape[1]

    @pl.loop(0, rows // 8)
    def _(i):
        here = row_chunk(i)
        values = [
            (
                field[0, here, a * RADIX : (a + 1) * RADIX],
                field[1, here, a * RADIX : (a + 1) * RADIX],
            )
            for a in range(INNER)
        ]
        for c, (re, im) in enumerate(butterflies(values, -1.0)):
            tr, ti = twist[0, c : c + 1, :], twist[1, c : c + 1, :]
            work[c, here, :RADIX] = re * tr - im * ti
            work[c, here, RADIX:] = re * ti + im * tr

    @pl.loop(0, INNER)
    def _(c):
        out[c] = right_product(work[c], table)


def move_rows(sense, data, factor, forward, backward, twist, out, work, spectrum):
    @pl.loop(0, RADIX // 8)
    def _(i):
        here = row_chunk(i)
        below = pl.ds(pl.multiple_of(RADIX + i * 8, 8), 8)
        values = [(data[a, here, :RADIX], data[a, here, RADIX:]) for a in range(INNER)]
        for c, (re, im) in enumerate(butterflies(values, -1.0)):
            tr, ti = twist[0, c, here, :], twist[1, c, here, :]
            side = slice((c % 2) * RADIX, (c % 2 + 1) * RADIX)
            work[c // 2, here, side] = re * tr - im * ti
            work[c // 2, below, side] = re * ti + im * tr

    @pl.loop(0, INNER // 2)
    def _(p):
        spectrum[p] = left_product(forward, work[p])

    for which in range(NREF):

        @pl.loop(0, INNER // 2)
        def _(p):
            re, im = spectrum[p, :RADIX, :], spectrum[p, RADIX:, :]
            fr, fi = factor[which, 0, p], sense * factor[which, 1, p]
            moved = jnp.concatenate([re * fr - im * fi, re * fi + im * fr], axis=0)
            work[p] = left_product(backward, moved)

        @pl.loop(0, RADIX // 8)
        def _(i):
            here = row_chunk(i)
            below = pl.ds(pl.multiple_of(RADIX + i * 8, 8), 8)
            values = []
            for c in range(INNER):
                side = slice((c % 2) * RADIX, (c % 2 + 1) * RADIX)
                re, im = work[c // 2, here, side], work[c // 2, below, side]
                tr, ti = twist[0, c, here, :], twist[1, c, here, :]
                values.append((re * tr + im * ti, im * tr - re * ti))
            for a, (re, im) in enumerate(butterflies(values, 1.0)):
                out[a, which, here, :RADIX] = re
                out[a, which, here, RADIX:] = im


def backward_columns(data, chosen, table, twist, out, work):
    rows = data.shape[2]
    for which in range(NREF):

        @pl.loop(0, INNER)
        def _(c):
            work[c] = right_product(data[c, which], table)

        @pl.loop(0, rows // 8)
        def _(i):
            here = row_chunk(i)
            values = []
            for c in range(INNER):
                re, im = work[c, here, :RADIX], work[c, here, RADIX:]
                tr, ti = twist[0, c : c + 1, :], twist[1, c : c + 1, :]
                values.append((re * tr + im * ti, im * tr - re * ti))
            for a, (re, im) in enumerate(butterflies(values, 1.0)):
                side = slice(a * RADIX, (a + 1) * RADIX)
                if which > 0:
                    mine = chosen[here, side] == which
                    re = jnp.where(mine, re, out[0, here, side])
                    im = jnp.where(mine, im, out[1, here, side])
                out[0, here, side] = re
                out[1, here, side] = im


def f32(*shape):
    return jax.ShapeDtypeStruct(shape, jnp.float32)


def cost(us_bytes):
    return pl.CostEstimate(flops=2 * 10**9, bytes_accessed=us_bytes, transcendentals=0)


def series(square, start):
    total = jnp.full_like(square, (-1.0) ** 10 / math.factorial(20 + start))
    for k in range(9, -1, -1):
        total = total * square + (-1.0) ** k / math.factorial(2 * k + start)
    return total


def per_device(
    source_field, rec_blocks, dest_device, dest_bin, slowness, ref_index, ref_slow, omega
):
    lanes = lax.axis_size("lat")
    rows = source_field.shape[2]
    columns = source_field.shape[3]
    width = rec_blocks.shape[3]
    fits = lanes == INNER and rows == RADIX and columns == LENGTH and width == RADIX
    if not fits or rec_blocks.shape[2] != 1 or source_field.shape[1] != 1:
        return general(
            source_field, rec_blocks, dest_device, dest_bin, slowness, ref_index, ref_slow, omega
        )
    me = lax.axis_index("lat")
    count = rec_blocks.shape[0]
    per_row = columns // width
    right_forward, right_backward = dft_tables(-1.0, False, 1.0), dft_tables(1.0, False, 1.0 / LENGTH)
    left_forward, left_backward = dft_tables(-1.0, True, 1.0), dft_tables(1.0, True, 1.0 / LENGTH)
    twist = jnp.asarray(twiddles(-1.0))
    wide_twist = jnp.broadcast_to(twist[:, :, :, None], (2, INNER, RADIX, RADIX))
    target = dest_device[:, 0] * (rows * per_row) + dest_bin
    packed = jnp.concatenate(
        [
            rec_blocks.reshape(count, 2 * width),
            jnp.broadcast_to(target.astype(jnp.float32)[:, None], (count, width)),
        ],
        axis=1,
    )
    packed = lax.all_gather(packed, "lat", axis=0, tiled=True)

    spectrum = pl.pallas_call(
        forward_columns,
        out_shape=f32(INNER, rows, 2 * RADIX),
        scratch_shapes=[pltpu.VMEM((INNER, rows, 2 * RADIX), jnp.float32)],
        compiler_params=PARAMS,
        cost_estimate=cost(2**23),
        name="forward_columns",
    )(source_field[:, 0], right_forward, twist)
    source_part = lax.all_to_all(spectrum, "lat", split_axis=0, concat_axis=0, tiled=True)

    step = 2.0 * math.pi / (LENGTH * SPACING) * DEPTH_STEP
    number = jnp.arange(LENGTH, dtype=jnp.int32)
    signed = jnp.where(number < LENGTH // 2, number, number - LENGTH).astype(jnp.float32) * step
    squares = (signed * signed).reshape(RADIX, INNER)
    kx_square = squares.T.reshape(INNER // 2, 2, RADIX).transpose(0, 2, 1)
    ky_square = lax.dynamic_slice_in_dim(squares, me, 1, axis=1)[:, 0]
    radial = (kx_square[:, :, :, None] + ky_square).reshape(INNER // 2, RADIX, 2 * RADIX)
    limit = (omega[0] * ref_slow[0] * DEPTH_STEP) ** 2
    argument = limit[:, None, None, None] - radial[None]
    inside = jnp.maximum(argument, 0.0)
    amplitude = jnp.exp(-jnp.sqrt(jnp.maximum(-argument, 0.0)))
    factor = jnp.stack(
        [
            amplitude * series(inside, 0),
            jnp.sign(omega[0]) * amplitude * jnp.sqrt(inside) * series(inside, 1),
        ],
        axis=1,
    )

    target = jnp.round(packed[:, 2 * width]).astype(jnp.int32)
    row, place = target // per_row, target % per_row
    own = lax.dynamic_slice_in_dim(twist, me, 1, axis=1)[:, 0]
    turn = (place * me % INNER).astype(jnp.float32) * (-2.0 * math.pi / INNER)
    turn_real, turn_imag = jnp.cos(turn)[:, None], jnp.sin(turn)[:, None]
    weight_real = turn_real * own[0] - turn_imag * own[1]
    weight_imag = turn_real * own[1] + turn_imag * own[0]
    real, imag = packed[:, :width], packed[:, width : 2 * width]
    turned = jnp.concatenate(
        [real * weight_real - imag * weight_imag, real * weight_imag + imag * weight_real], axis=1
    )
    whole_table = right_forward[0].astype(jnp.float32) + right_forward[1].astype(jnp.float32)
    traces = jnp.dot(turned, whole_table, precision=lax.Precision.HIGHEST)
    spread = (jnp.arange(lanes * rows, dtype=jnp.int32)[:, None] == row[None, :]).astype(jnp.float32)
    received_part = jnp.dot(spread, traces, precision=lax.Precision.HIGHEST)
    received_part = received_part.reshape(INNER, RADIX, 2 * RADIX)

    def propagate(part, sense, label):
        moved = pl.pallas_call(
            partial(move_rows, sense),
            out_shape=f32(INNER, NREF, RADIX, 2 * RADIX),
            scratch_shapes=[
                pltpu.VMEM((INNER // 2, 2 * RADIX, 2 * RADIX), jnp.float32),
                pltpu.VMEM((INNER // 2, 2 * RADIX, 2 * RADIX), jnp.float32),
            ],
            compiler_params=PARAMS,
            cost_estimate=cost(2**25),
            name="move_rows_" + label,
        )(part, factor, left_forward, left_backward, wide_twist)
        return lax.all_to_all(moved, "lat", split_axis=0, concat_axis=0, tiled=True)

    chosen = ref_index[0]

    def restore(back, label):
        return pl.pallas_call(
            backward_columns,
            out_shape=f32(2, rows, columns),
            scratch_shapes=[pltpu.VMEM((INNER, rows, 2 * RADIX), jnp.float32)],
            compiler_params=PARAMS,
            cost_estimate=cost(2**24),
            name="backward_columns_" + label,
        )(back, chosen, right_backward, twist)

    received = restore(propagate(received_part, 1.0, "received"), "received")
    source = restore(propagate(source_part, -1.0, "source"), "source")
    speed = jnp.where(chosen == 1, ref_slow[0, 1], ref_slow[0, 0])
    double = (2.0 * DEPTH_STEP) * omega[0] * (slowness[0] - speed)
    square = double * double
    cosine, sine = series(square, 0), double * series(square, 1)
    cross_real = source[0] * received[0] + source[1] * received[1]
    cross_imag = source[1] * received[0] - source[0] * received[1]
    return (cross_real * cosine + cross_imag * sine)[None]


def solution(mesh):
    return jax.shard_map(
        per_device,
        mesh=mesh,
        in_specs=(
            P(None, "shots", "lat", None),
            P(("shots", "lat"), None, None, None),
            P(("shots", "lat"), None),
            P(("shots", "lat")),
            P(None, "lat", None),
            P(None, "lat", None),
            P(),
            P(),
        ),
        out_specs=P("shots", "lat", None),
        check_vma=False,
    )
```

```python
from functools import partial
import math

import jax
import jax.numpy as jnp
import numpy as np
from jax import lax
from jax.experimental import pallas as pl
from jax.experimental.pallas import tpu as pltpu
from jax.sharding import PartitionSpec as P

NREF = 2
CAP = 2


SPACING = 0.01
DEPTH_STEP = 0.01
RADIX = 128


def angle_table(size, direction):
    index = jnp.arange(size, dtype=jnp.int32)
    product = index[:, None] * index[None, :] % size
    angle = direction * 2.0 * math.pi * product.astype(jnp.float32) / size
    return (jnp.cos(angle), jnp.sin(angle))


def twist_table(length, direction):
    outer_index = jnp.arange(length // RADIX, dtype=jnp.int32)
    radix_index = jnp.arange(RADIX, dtype=jnp.int32)
    product = outer_index[:, None] * radix_index[None, :] % length
    angle = direction * 2.0 * math.pi * product.astype(jnp.float32) / length
    return (jnp.cos(angle), jnp.sin(angle))


def complex_einsum(formula, real_in, imag_in, real_mat, imag_mat):
    multiply = partial(jnp.einsum, formula, precision=lax.Precision.HIGHEST)
    return (
        multiply(real_in, real_mat) - multiply(imag_in, imag_mat),
        multiply(real_in, imag_mat) + multiply(imag_in, real_mat),
    )


def transform(real_in, imag_in, trailing, direction):
    length = real_in.shape[-2] if trailing else real_in.shape[-1]
    inner = length // RADIX
    first_real, first_imag = angle_table(inner, direction)
    second_real, second_imag = angle_table(RADIX, direction)
    twist_real, twist_imag = twist_table(length, direction)
    initial = real_in.shape
    if trailing:
        shape = initial[:-2] + (inner, RADIX, initial[-1])
        twist_real = twist_real[:, :, None]
        twist_imag = twist_imag[:, :, None]
        tail = "z"
    else:
        shape = initial[:-1] + (inner, RADIX)
        tail = ""
    work_real = real_in.reshape(shape)
    work_imag = imag_in.reshape(shape)
    if direction < 0:
        work_real, work_imag = complex_einsum(
            "...ab" + tail + ",ac->...cb" + tail, work_real, work_imag, first_real, first_imag
        )
        work_real, work_imag = (
            work_real * twist_real - work_imag * twist_imag,
            work_real * twist_imag + work_imag * twist_real,
        )
        work_real, work_imag = complex_einsum(
            "...cb" + tail + ",bd->...cd" + tail, work_real, work_imag, second_real, second_imag
        )
    else:
        work_real, work_imag = complex_einsum(
            "...cb" + tail + ",bd->...cd" + tail, work_real, work_imag, second_real, second_imag
        )
        work_real, work_imag = (
            work_real * twist_real - work_imag * twist_imag,
            work_real * twist_imag + work_imag * twist_real,
        )
        work_real, work_imag = complex_einsum(
            "...cb" + tail + ",ca->...ab" + tail, work_real, work_imag, first_real, first_imag
        )
        work_real = work_real / length
        work_imag = work_imag / length
    return (work_real.reshape(initial), work_imag.reshape(initial))


def permuted_numbers(positions, length):
    inner = length // RADIX
    index = positions // RADIX + inner * (positions % RADIX)
    signed = jnp.where(index < length // 2, index, index - length)
    return signed.astype(jnp.float32) * (2.0 * math.pi / (length * SPACING))


def general(
    source_field, rec_blocks, dest_device, dest_bin, slowness, ref_index, ref_slow, omega
):
    lanes = lax.axis_size("lat")
    count_blocks = rec_blocks.shape[0]
    freqs = rec_blocks.shape[2]
    block_width = rec_blocks.shape[3]
    rows_here = source_field.shape[2]
    columns = source_field.shape[3]
    bins_here = rows_here * (columns // block_width)
    slots = lanes * CAP
    flat = rec_blocks.reshape(count_blocks, 2 * freqs * block_width)
    onehot = (dest_device == jnp.arange(lanes, dtype=jnp.int32)[None, :]).astype(jnp.int32)
    order = jnp.arange(count_blocks, dtype=jnp.int32)
    before = (order[None, :] < order[:, None]).astype(jnp.int32)
    earlier = jnp.sum(before[:, :, None] * onehot[None, :, :], axis=1)
    ranking = jnp.sum(onehot * earlier, axis=1)
    slot_of = dest_device[:, 0] * CAP + ranking
    placing = slot_of[None, :] == jnp.arange(slots, dtype=jnp.int32)[:, None]
    outgoing = jnp.dot(placing.astype(jnp.float32), flat, precision=lax.Precision.HIGHEST)
    labels = jnp.sum(jnp.where(placing, (dest_bin + 1)[None, :], 0), axis=1).astype(jnp.float32)
    arrived, arrived_labels = (
        lax.all_to_all(
            outgoing.reshape(lanes, CAP, -1), "lat", split_axis=0, concat_axis=0, tiled=True
        ),
        lax.all_to_all(labels.reshape(lanes, CAP), "lat", split_axis=0, concat_axis=0, tiled=True),
    )
    bin_labels = arrived_labels.reshape(slots).astype(jnp.int32) - 1
    gathering = (bin_labels[None, :] == jnp.arange(bins_here, dtype=jnp.int32)[:, None]).astype(
        jnp.float32
    )
    binned = jnp.dot(gathering, arrived.reshape(slots, -1), precision=lax.Precision.HIGHEST)
    binned = binned.reshape(rows_here, columns // block_width, 2, freqs, block_width)
    received = binned.transpose(2, 3, 0, 1, 4).reshape(2, freqs, rows_here, columns)
    field_real = jnp.concatenate([source_field[0], received[0]], axis=0)
    field_imag = jnp.concatenate([source_field[1], received[1]], axis=0)
    signed = jnp.concatenate([-omega, omega])
    spec_real, spec_imag = transform(field_real, field_imag, False, -1.0)
    carried = jnp.broadcast_to(signed[:, None, None], (2 * freqs, 1, lanes))
    part_real = lax.all_to_all(spec_real, "lat", split_axis=2, concat_axis=1, tiled=True)
    part_imag = lax.all_to_all(spec_imag, "lat", split_axis=2, concat_axis=1, tiled=True)
    part_params = lax.all_to_all(carried, "lat", split_axis=2, concat_axis=1, tiled=True)
    total_rows = part_real.shape[1]
    local_cols = part_real.shape[2]
    freq_real, freq_imag = transform(part_real, part_imag, True, -1.0)
    kx_values = permuted_numbers(jnp.arange(total_rows, dtype=jnp.int32), total_rows)
    positions = lax.axis_index("lat") * local_cols + jnp.arange(local_cols, dtype=jnp.int32)
    ky_values = permuted_numbers(positions, lanes * local_cols)
    radial = kx_values[:, None] ** 2 + ky_values[None, :] ** 2
    freq_signed = part_params[:, 0, 0]
    sense = jnp.sign(freq_signed)[:, None, None]
    shifted_real = []
    shifted_imag = []
    for propagate_which in range(NREF):
        propagate_speed = ref_slow[0, propagate_which]
        argument = (freq_signed**2)[:, None, None] * propagate_speed**2 - radial[None]
        amplitude = jnp.exp(-jnp.sqrt(jnp.maximum(-argument, 0.0)) * DEPTH_STEP)
        phase = sense * jnp.sqrt(jnp.maximum(argument, 0.0)) * DEPTH_STEP
        factor_real = amplitude * jnp.cos(phase)
        factor_imag = amplitude * jnp.sin(phase)
        moved_real = freq_real * factor_real - freq_imag * factor_imag
        moved_imag = freq_real * factor_imag + freq_imag * factor_real
        moved_real, moved_imag = transform(moved_real, moved_imag, True, 1.0)
        shifted_real.append(moved_real)
        shifted_imag.append(moved_imag)
    stacked_real = jnp.stack(shifted_real, axis=1)
    stacked_imag = jnp.stack(shifted_imag, axis=1)
    back_real = lax.all_to_all(stacked_real, "lat", split_axis=2, concat_axis=3, tiled=True)
    back_imag = lax.all_to_all(stacked_imag, "lat", split_axis=2, concat_axis=3, tiled=True)
    space_real, space_imag = transform(back_real, back_imag, False, 1.0)
    new_real = jnp.zeros_like(field_real)
    new_imag = jnp.zeros_like(field_imag)
    for which in range(NREF):
        speed = ref_slow[0, which]
        angle = signed[:, None, None] * (slowness[0] - speed)[None] * DEPTH_STEP
        cosine = jnp.cos(angle)
        sine = jnp.sin(angle)
        fixed_real = space_real[:, which] * cosine - space_imag[:, which] * sine
        fixed_imag = space_real[:, which] * sine + space_imag[:, which] * cosine
        chosen = (ref_index[0] == which)[None]
        new_real = jnp.where(chosen, fixed_real, new_real)
        new_imag = jnp.where(chosen, fixed_imag, new_imag)
    images = [
        jnp.sum(new_real[:freqs] * new_real[freqs:] + new_imag[:freqs] * new_imag[freqs:], axis=0)
    ]
    return jnp.stack(images)


INNER = 16
LENGTH = INNER * RADIX
PARAMS = pltpu.CompilerParams(vmem_limit_bytes=50 * 2**20)


def dft_tables(direction, left, scale):
    index = np.arange(RADIX)
    angle = direction * 2.0 * np.pi * (index[:, None] * index[None, :] % RADIX) / RADIX
    cosine, sine = np.cos(angle) * scale, np.sin(angle) * scale
    whole = np.block([[cosine, -sine], [sine, cosine]] if left else [[cosine, sine], [-sine, cosine]])
    whole = jnp.asarray(whole.astype(np.float32))
    high = whole.astype(jnp.bfloat16)
    low = (whole - high.astype(jnp.float32)).astype(jnp.bfloat16)
    return jnp.stack([high, low])


def twiddles(direction):
    angle = direction * 2.0 * np.pi * (np.arange(INNER)[:, None] * np.arange(RADIX)[None, :]) / LENGTH
    return np.stack([np.cos(angle), np.sin(angle)]).astype(np.float32)


def butterflies(values, direction):
    count = len(values)
    if count == 1:
        return values
    even = butterflies(values[0::2], direction)
    odd = butterflies(values[1::2], direction)
    first, second = [], []
    for k in range(count // 2):
        (er, ei), (pr, pi) = even[k], odd[k]
        if k == 0:
            tr, ti = pr, pi
        elif 4 * k == count:
            tr, ti = (-pi, pr) if direction > 0 else (pi, -pr)
        else:
            c = math.cos(2.0 * math.pi * k / count)
            d = direction * math.sin(2.0 * math.pi * k / count)
            tr, ti = pr * c - pi * d, pr * d + pi * c
        first.append((er + tr, ei + ti))
        second.append((er - tr, ei - ti))
    return first + second


def halves(value):
    high = value.astype(jnp.bfloat16)
    return high, (value - high.astype(jnp.float32)).astype(jnp.bfloat16)


def mul(a, b):
    return jnp.dot(a, b, preferred_element_type=jnp.float32)


def right_product(value, table):
    high, low = halves(value)
    return mul(low, table[0]) + mul(high, table[1]) + mul(high, table[0])


def left_product(table, value):
    high, low = halves(value)
    return mul(table[1], high) + mul(table[0], low) + mul(table[0], high)


def row_chunk(i):
    return pl.ds(pl.multiple_of(i * 8, 8), 8)


def forward_columns(field, table, twist, out, work):
    rows = field.shape[1]

    @pl.loop(0, rows // 8)
    def _(i):
        here = row_chunk(i)
        values = [
            (
                field[0, here, a * RADIX : (a + 1) * RADIX],
                field[1, here, a * RADIX : (a + 1) * RADIX],
            )
            for a in range(INNER)
        ]
        for c, (re, im) in enumerate(butterflies(values, -1.0)):
            tr, ti = twist[0, c : c + 1, :], twist[1, c : c + 1, :]
            work[c, here, :RADIX] = re * tr - im * ti
            work[c, here, RADIX:] = re * ti + im * tr

    @pl.loop(0, INNER)
    def _(c):
        out[c] = right_product(work[c], table)


def move_rows(sense, data, factor, forward, backward, twist, out, work, spectrum):
    @pl.loop(0, RADIX // 8)
    def _(i):
        here = row_chunk(i)
        below = pl.ds(pl.multiple_of(RADIX + i * 8, 8), 8)
        values = [(data[a, here, :RADIX], data[a, here, RADIX:]) for a in range(INNER)]
        for c, (re, im) in enumerate(butterflies(values, -1.0)):
            tr, ti = twist[0, c, here, :], twist[1, c, here, :]
            side = slice((c % 2) * RADIX, (c % 2 + 1) * RADIX)
            work[c // 2, here, side] = re * tr - im * ti
            work[c // 2, below, side] = re * ti + im * tr

    @pl.loop(0, INNER // 2)
    def _(p):
        spectrum[p] = left_product(forward, work[p])

    for which in range(NREF):

        @pl.loop(0, INNER // 2)
        def _(p):
            re, im = spectrum[p, :RADIX, :], spectrum[p, RADIX:, :]
            fr, fi = factor[which, 0, p], sense * factor[which, 1, p]
            moved = jnp.concatenate([re * fr - im * fi, re * fi + im * fr], axis=0)
            work[p] = left_product(backward, moved)

        @pl.loop(0, RADIX // 8)
        def _(i):
            here = row_chunk(i)
            below = pl.ds(pl.multiple_of(RADIX + i * 8, 8), 8)
            values = []
            for c in range(INNER):
                side = slice((c % 2) * RADIX, (c % 2 + 1) * RADIX)
                re, im = work[c // 2, here, side], work[c // 2, below, side]
                tr, ti = twist[0, c, here, :], twist[1, c, here, :]
                values.append((re * tr + im * ti, im * tr - re * ti))
            for a, (re, im) in enumerate(butterflies(values, 1.0)):
                out[a, which, here, :RADIX] = re
                out[a, which, here, RADIX:] = im


def backward_columns(data, chosen, table, twist, *rest):
    other, out, work, keep = rest if len(rest) == 4 else (None, *rest)
    rows = data.shape[2]
    for which in range(NREF):
        flat = data[:, which].reshape(INNER * rows, 2 * RADIX)
        work[...] = right_product(flat, table).reshape(INNER, rows, 2 * RADIX)

        @pl.loop(0, rows // 8)
        def _(i):
            here = row_chunk(i)
            values = []
            for c in range(INNER):
                re, im = work[c, here, :RADIX], work[c, here, RADIX:]
                tr, ti = twist[0, c : c + 1, :], twist[1, c : c + 1, :]
                values.append((re * tr + im * ti, im * tr - re * ti))
            for a, (re, im) in enumerate(butterflies(values, 1.0)):
                side = slice(a * RADIX, (a + 1) * RADIX)
                if which > 0:
                    mine = chosen[here, side] == which
                    re = jnp.where(mine, re, keep[0, here, side])
                    im = jnp.where(mine, im, keep[1, here, side])
                if which < NREF - 1:
                    keep[0, here, side] = re
                    keep[1, here, side] = im
                elif other is None:
                    out[0, here, side] = re
                    out[1, here, side] = im
                else:
                    out[here, side] = other[0, here, side] * re + other[1, here, side] * im


def f32(*shape):
    return jax.ShapeDtypeStruct(shape, jnp.float32)


def cost(us_bytes):
    return pl.CostEstimate(flops=2 * 10**9, bytes_accessed=us_bytes, transcendentals=0)


def series(square, start):
    total = jnp.full_like(square, (-1.0) ** 10 / math.factorial(20 + start))
    for k in range(9, -1, -1):
        total = total * square + (-1.0) ** k / math.factorial(2 * k + start)
    return total


def per_device(
    source_field, rec_blocks, dest_device, dest_bin, slowness, ref_index, ref_slow, omega
):
    lanes = lax.axis_size("lat")
    rows = source_field.shape[2]
    columns = source_field.shape[3]
    width = rec_blocks.shape[3]
    fits = lanes == INNER and rows == RADIX and columns == LENGTH and width == RADIX
    if not fits or rec_blocks.shape[2] != 1 or source_field.shape[1] != 1:
        return general(
            source_field, rec_blocks, dest_device, dest_bin, slowness, ref_index, ref_slow, omega
        )
    me = lax.axis_index("lat")
    count = rec_blocks.shape[0]
    per_row = columns // width
    right_forward, right_backward = dft_tables(-1.0, False, 1.0), dft_tables(1.0, False, 1.0 / LENGTH)
    left_forward, left_backward = dft_tables(-1.0, True, 1.0), dft_tables(1.0, True, 1.0 / LENGTH)
    twist = jnp.asarray(twiddles(-1.0))
    wide_twist = jnp.broadcast_to(twist[:, :, :, None], (2, INNER, RADIX, RADIX))
    target = dest_device[:, 0] * (rows * per_row) + dest_bin
    packed = jnp.concatenate(
        [
            rec_blocks.reshape(count, 2 * width),
            jnp.broadcast_to(target.astype(jnp.float32)[:, None], (count, width)),
        ],
        axis=1,
    )
    spectrum = pl.pallas_call(
        forward_columns,
        out_shape=f32(INNER, rows, 2 * RADIX),
        scratch_shapes=[pltpu.VMEM((INNER, rows, 2 * RADIX), jnp.float32)],
        compiler_params=PARAMS,
        cost_estimate=cost(2**23),
        name="forward_columns",
    )(source_field[:, 0], right_forward, twist)
    source_part = lax.all_to_all(spectrum, "lat", split_axis=0, concat_axis=0, tiled=True)
    packed, source_part = lax.optimization_barrier((packed, source_part))
    copies = jnp.broadcast_to(packed[None], (lanes,) + packed.shape)
    packed = lax.all_to_all(copies, "lat", split_axis=0, concat_axis=0, tiled=True)
    packed = packed.reshape(lanes * count, 3 * width)

    step = 2.0 * math.pi / (LENGTH * SPACING) * DEPTH_STEP
    number = jnp.arange(LENGTH, dtype=jnp.int32)
    signed = jnp.where(number < LENGTH // 2, number, number - LENGTH).astype(jnp.float32) * step
    squares = (signed * signed).reshape(RADIX, INNER)
    kx_square = squares.T.reshape(INNER // 2, 2, RADIX).transpose(0, 2, 1)
    ky_square = lax.dynamic_slice_in_dim(squares, me, 1, axis=1)[:, 0]
    radial = (kx_square[:, :, :, None] + ky_square).reshape(INNER // 2, RADIX, 2 * RADIX)
    limit = (omega[0] * ref_slow[0] * DEPTH_STEP) ** 2
    argument = limit[:, None, None, None] - radial[None]
    inside = jnp.maximum(argument, 0.0)
    amplitude = jnp.exp(-jnp.sqrt(jnp.maximum(-argument, 0.0)))
    factor = jnp.stack(
        [
            amplitude * series(inside, 0),
            jnp.sign(omega[0]) * amplitude * jnp.sqrt(inside) * series(inside, 1),
        ],
        axis=1,
    )

    def propagate(part, sense, label):
        return pl.pallas_call(
            partial(move_rows, sense),
            out_shape=f32(INNER, NREF, RADIX, 2 * RADIX),
            scratch_shapes=[
                pltpu.VMEM((INNER // 2, 2 * RADIX, 2 * RADIX), jnp.float32),
                pltpu.VMEM((INNER // 2, 2 * RADIX, 2 * RADIX), jnp.float32),
            ],
            compiler_params=PARAMS,
            cost_estimate=cost(2**25),
            name="move_rows_" + label,
        )(part, factor, left_forward, left_backward, wide_twist)

    def send_back(moved):
        return lax.all_to_all(moved, "lat", split_axis=0, concat_axis=0, tiled=True)

    packed, moved = lax.optimization_barrier((packed, propagate(source_part, -1.0, "source")))
    source_back = send_back(moved)

    target = jnp.round(packed[:, 2 * width]).astype(jnp.int32)
    row, place = target // per_row, target % per_row
    own = lax.dynamic_slice_in_dim(twist, me, 1, axis=1)[:, 0]
    turn = (place * me % INNER).astype(jnp.float32) * (-2.0 * math.pi / INNER)
    turn_real, turn_imag = jnp.cos(turn)[:, None], jnp.sin(turn)[:, None]
    weight_real = turn_real * own[0] - turn_imag * own[1]
    weight_imag = turn_real * own[1] + turn_imag * own[0]
    real, imag = packed[:, :width], packed[:, width : 2 * width]
    turned = jnp.concatenate(
        [real * weight_real - imag * weight_imag, real * weight_imag + imag * weight_real], axis=1
    )
    whole_table = right_forward[0].astype(jnp.float32) + right_forward[1].astype(jnp.float32)
    traces = jnp.dot(turned, whole_table, precision=lax.Precision.HIGHEST)
    spread = (jnp.arange(lanes * rows, dtype=jnp.int32)[:, None] == row[None, :]).astype(jnp.float32)
    received_part = jnp.dot(spread, traces, precision=lax.Precision.HIGHEST)
    received_part = received_part.reshape(INNER, RADIX, 2 * RADIX)

    chosen = ref_index[0]

    share = rows // 4

    def restore(back, label, *other):
        fields = pl.BlockSpec((2, share, columns), lambda i: (0, i, 0))
        plane = pl.BlockSpec((share, columns), lambda i: (i, 0))
        return pl.pallas_call(
            backward_columns,
            grid=(rows // share,),
            in_specs=[
                pl.BlockSpec((INNER, NREF, share, 2 * RADIX), lambda i: (0, 0, i, 0)),
                plane,
                pl.BlockSpec((2, 2 * RADIX, 2 * RADIX), lambda i: (0, 0, 0)),
                pl.BlockSpec((2, INNER, RADIX), lambda i: (0, 0, 0)),
            ]
            + [fields] * len(other),
            out_specs=plane if other else fields,
            out_shape=f32(rows, columns) if other else f32(2, rows, columns),
            scratch_shapes=[
                pltpu.VMEM((INNER, share, 2 * RADIX), jnp.float32),
                pltpu.VMEM((2, share, columns), jnp.float32),
            ],
            compiler_params=PARAMS,
            cost_estimate=cost(2**24),
            name="backward_columns_" + label,
        )(back, chosen, right_backward, twist, *other)

    received_back = send_back(propagate(received_part, 1.0, "received"))
    source = restore(source_back, "source")
    speed = jnp.where(chosen == 1, ref_slow[0, 1], ref_slow[0, 0])
    double = (2.0 * DEPTH_STEP) * omega[0] * (slowness[0] - speed)
    square = double * double
    cosine, sine = series(square, 0), double * series(square, 1)
    turned_source = jnp.stack(
        [source[0] * cosine + source[1] * sine, source[1] * cosine - source[0] * sine]
    )
    return restore(received_back, "image", turned_source)[None]


def solution(mesh):
    return jax.shard_map(
        per_device,
        mesh=mesh,
        in_specs=(
            P(None, "shots", "lat", None),
            P(("shots", "lat"), None, None, None),
            P(("shots", "lat"), None),
            P(("shots", "lat")),
            P(None, "lat", None),
            P(None, "lat", None),
            P(),
            P(),
        ),
        out_specs=P("shots", "lat", None),
        check_vma=False,
    )
```

```python
from functools import partial
import math

import jax
import jax.numpy as jnp
import numpy as np
from jax import lax
from jax.experimental import pallas as pl
from jax.experimental.pallas import tpu as pltpu
from jax.sharding import PartitionSpec as P

NREF = 2
CAP = 2


SPACING = 0.01
DEPTH_STEP = 0.01
RADIX = 128


def angle_table(size, direction):
    index = jnp.arange(size, dtype=jnp.int32)
    product = index[:, None] * index[None, :] % size
    angle = direction * 2.0 * math.pi * product.astype(jnp.float32) / size
    return (jnp.cos(angle), jnp.sin(angle))


def twist_table(length, direction):
    outer_index = jnp.arange(length // RADIX, dtype=jnp.int32)
    radix_index = jnp.arange(RADIX, dtype=jnp.int32)
    product = outer_index[:, None] * radix_index[None, :] % length
    angle = direction * 2.0 * math.pi * product.astype(jnp.float32) / length
    return (jnp.cos(angle), jnp.sin(angle))


def complex_einsum(formula, real_in, imag_in, real_mat, imag_mat):
    multiply = partial(jnp.einsum, formula, precision=lax.Precision.HIGHEST)
    return (
        multiply(real_in, real_mat) - multiply(imag_in, imag_mat),
        multiply(real_in, imag_mat) + multiply(imag_in, real_mat),
    )


def transform(real_in, imag_in, trailing, direction):
    length = real_in.shape[-2] if trailing else real_in.shape[-1]
    inner = length // RADIX
    first_real, first_imag = angle_table(inner, direction)
    second_real, second_imag = angle_table(RADIX, direction)
    twist_real, twist_imag = twist_table(length, direction)
    initial = real_in.shape
    if trailing:
        shape = initial[:-2] + (inner, RADIX, initial[-1])
        twist_real = twist_real[:, :, None]
        twist_imag = twist_imag[:, :, None]
        tail = "z"
    else:
        shape = initial[:-1] + (inner, RADIX)
        tail = ""
    work_real = real_in.reshape(shape)
    work_imag = imag_in.reshape(shape)
    if direction < 0:
        work_real, work_imag = complex_einsum(
            "...ab" + tail + ",ac->...cb" + tail, work_real, work_imag, first_real, first_imag
        )
        work_real, work_imag = (
            work_real * twist_real - work_imag * twist_imag,
            work_real * twist_imag + work_imag * twist_real,
        )
        work_real, work_imag = complex_einsum(
            "...cb" + tail + ",bd->...cd" + tail, work_real, work_imag, second_real, second_imag
        )
    else:
        work_real, work_imag = complex_einsum(
            "...cb" + tail + ",bd->...cd" + tail, work_real, work_imag, second_real, second_imag
        )
        work_real, work_imag = (
            work_real * twist_real - work_imag * twist_imag,
            work_real * twist_imag + work_imag * twist_real,
        )
        work_real, work_imag = complex_einsum(
            "...cb" + tail + ",ca->...ab" + tail, work_real, work_imag, first_real, first_imag
        )
        work_real = work_real / length
        work_imag = work_imag / length
    return (work_real.reshape(initial), work_imag.reshape(initial))


def permuted_numbers(positions, length):
    inner = length // RADIX
    index = positions // RADIX + inner * (positions % RADIX)
    signed = jnp.where(index < length // 2, index, index - length)
    return signed.astype(jnp.float32) * (2.0 * math.pi / (length * SPACING))


def general(
    source_field, rec_blocks, dest_device, dest_bin, slowness, ref_index, ref_slow, omega
):
    lanes = lax.axis_size("lat")
    count_blocks = rec_blocks.shape[0]
    freqs = rec_blocks.shape[2]
    block_width = rec_blocks.shape[3]
    rows_here = source_field.shape[2]
    columns = source_field.shape[3]
    bins_here = rows_here * (columns // block_width)
    slots = lanes * CAP
    flat = rec_blocks.reshape(count_blocks, 2 * freqs * block_width)
    onehot = (dest_device == jnp.arange(lanes, dtype=jnp.int32)[None, :]).astype(jnp.int32)
    order = jnp.arange(count_blocks, dtype=jnp.int32)
    before = (order[None, :] < order[:, None]).astype(jnp.int32)
    earlier = jnp.sum(before[:, :, None] * onehot[None, :, :], axis=1)
    ranking = jnp.sum(onehot * earlier, axis=1)
    slot_of = dest_device[:, 0] * CAP + ranking
    placing = slot_of[None, :] == jnp.arange(slots, dtype=jnp.int32)[:, None]
    outgoing = jnp.dot(placing.astype(jnp.float32), flat, precision=lax.Precision.HIGHEST)
    labels = jnp.sum(jnp.where(placing, (dest_bin + 1)[None, :], 0), axis=1).astype(jnp.float32)
    arrived, arrived_labels = (
        lax.all_to_all(
            outgoing.reshape(lanes, CAP, -1), "lat", split_axis=0, concat_axis=0, tiled=True
        ),
        lax.all_to_all(labels.reshape(lanes, CAP), "lat", split_axis=0, concat_axis=0, tiled=True),
    )
    bin_labels = arrived_labels.reshape(slots).astype(jnp.int32) - 1
    gathering = (bin_labels[None, :] == jnp.arange(bins_here, dtype=jnp.int32)[:, None]).astype(
        jnp.float32
    )
    binned = jnp.dot(gathering, arrived.reshape(slots, -1), precision=lax.Precision.HIGHEST)
    binned = binned.reshape(rows_here, columns // block_width, 2, freqs, block_width)
    received = binned.transpose(2, 3, 0, 1, 4).reshape(2, freqs, rows_here, columns)
    field_real = jnp.concatenate([source_field[0], received[0]], axis=0)
    field_imag = jnp.concatenate([source_field[1], received[1]], axis=0)
    signed = jnp.concatenate([-omega, omega])
    spec_real, spec_imag = transform(field_real, field_imag, False, -1.0)
    carried = jnp.broadcast_to(signed[:, None, None], (2 * freqs, 1, lanes))
    part_real = lax.all_to_all(spec_real, "lat", split_axis=2, concat_axis=1, tiled=True)
    part_imag = lax.all_to_all(spec_imag, "lat", split_axis=2, concat_axis=1, tiled=True)
    part_params = lax.all_to_all(carried, "lat", split_axis=2, concat_axis=1, tiled=True)
    total_rows = part_real.shape[1]
    local_cols = part_real.shape[2]
    freq_real, freq_imag = transform(part_real, part_imag, True, -1.0)
    kx_values = permuted_numbers(jnp.arange(total_rows, dtype=jnp.int32), total_rows)
    positions = lax.axis_index("lat") * local_cols + jnp.arange(local_cols, dtype=jnp.int32)
    ky_values = permuted_numbers(positions, lanes * local_cols)
    radial = kx_values[:, None] ** 2 + ky_values[None, :] ** 2
    freq_signed = part_params[:, 0, 0]
    sense = jnp.sign(freq_signed)[:, None, None]
    shifted_real = []
    shifted_imag = []
    for propagate_which in range(NREF):
        propagate_speed = ref_slow[0, propagate_which]
        argument = (freq_signed**2)[:, None, None] * propagate_speed**2 - radial[None]
        amplitude = jnp.exp(-jnp.sqrt(jnp.maximum(-argument, 0.0)) * DEPTH_STEP)
        phase = sense * jnp.sqrt(jnp.maximum(argument, 0.0)) * DEPTH_STEP
        factor_real = amplitude * jnp.cos(phase)
        factor_imag = amplitude * jnp.sin(phase)
        moved_real = freq_real * factor_real - freq_imag * factor_imag
        moved_imag = freq_real * factor_imag + freq_imag * factor_real
        moved_real, moved_imag = transform(moved_real, moved_imag, True, 1.0)
        shifted_real.append(moved_real)
        shifted_imag.append(moved_imag)
    stacked_real = jnp.stack(shifted_real, axis=1)
    stacked_imag = jnp.stack(shifted_imag, axis=1)
    back_real = lax.all_to_all(stacked_real, "lat", split_axis=2, concat_axis=3, tiled=True)
    back_imag = lax.all_to_all(stacked_imag, "lat", split_axis=2, concat_axis=3, tiled=True)
    space_real, space_imag = transform(back_real, back_imag, False, 1.0)
    new_real = jnp.zeros_like(field_real)
    new_imag = jnp.zeros_like(field_imag)
    for which in range(NREF):
        speed = ref_slow[0, which]
        angle = signed[:, None, None] * (slowness[0] - speed)[None] * DEPTH_STEP
        cosine = jnp.cos(angle)
        sine = jnp.sin(angle)
        fixed_real = space_real[:, which] * cosine - space_imag[:, which] * sine
        fixed_imag = space_real[:, which] * sine + space_imag[:, which] * cosine
        chosen = (ref_index[0] == which)[None]
        new_real = jnp.where(chosen, fixed_real, new_real)
        new_imag = jnp.where(chosen, fixed_imag, new_imag)
    images = [
        jnp.sum(new_real[:freqs] * new_real[freqs:] + new_imag[:freqs] * new_imag[freqs:], axis=0)
    ]
    return jnp.stack(images)


INNER = 16
LENGTH = INNER * RADIX
PARAMS = pltpu.CompilerParams(vmem_limit_bytes=50 * 2**20)


def dft_tables(direction, left, scale):
    index = np.arange(RADIX)
    angle = direction * 2.0 * np.pi * (index[:, None] * index[None, :] % RADIX) / RADIX
    cosine, sine = np.cos(angle) * scale, np.sin(angle) * scale
    whole = np.block([[cosine, -sine], [sine, cosine]] if left else [[cosine, sine], [-sine, cosine]])
    whole = jnp.asarray(whole.astype(np.float32))
    high = whole.astype(jnp.bfloat16)
    low = (whole - high.astype(jnp.float32)).astype(jnp.bfloat16)
    return jnp.stack([high, low])


def twiddles(direction):
    angle = direction * 2.0 * np.pi * (np.arange(INNER)[:, None] * np.arange(RADIX)[None, :]) / LENGTH
    return np.stack([np.cos(angle), np.sin(angle)]).astype(np.float32)


def butterflies(values, direction):
    count = len(values)
    if count == 1:
        return values
    even = butterflies(values[0::2], direction)
    odd = butterflies(values[1::2], direction)
    first, second = [], []
    for k in range(count // 2):
        (er, ei), (pr, pi) = even[k], odd[k]
        if k == 0:
            tr, ti = pr, pi
        elif 4 * k == count:
            tr, ti = (-pi, pr) if direction > 0 else (pi, -pr)
        else:
            c = math.cos(2.0 * math.pi * k / count)
            d = direction * math.sin(2.0 * math.pi * k / count)
            tr, ti = pr * c - pi * d, pr * d + pi * c
        first.append((er + tr, ei + ti))
        second.append((er - tr, ei - ti))
    return first + second


def halves(value):
    high = value.astype(jnp.bfloat16)
    return high, (value - high.astype(jnp.float32)).astype(jnp.bfloat16)


def mul(a, b):
    return jnp.dot(a, b, preferred_element_type=jnp.float32)


def right_product(value, table):
    high, low = halves(value)
    return mul(low, table[0]) + mul(high, table[1]) + mul(high, table[0])


def left_product(table, value):
    high, low = halves(value)
    return mul(table[1], high) + mul(table[0], low) + mul(table[0], high)


def row_chunk(i):
    return pl.ds(pl.multiple_of(i * 8, 8), 8)


def forward_columns(field, table, twist, out, work):
    rows = field.shape[1]

    @pl.loop(0, rows // 8)
    def _(i):
        here = row_chunk(i)
        values = [
            (
                field[0, here, a * RADIX : (a + 1) * RADIX],
                field[1, here, a * RADIX : (a + 1) * RADIX],
            )
            for a in range(INNER)
        ]
        for c, (re, im) in enumerate(butterflies(values, -1.0)):
            tr, ti = twist[0, c : c + 1, :], twist[1, c : c + 1, :]
            work[c, here, :RADIX] = re * tr - im * ti
            work[c, here, RADIX:] = re * ti + im * tr

    @pl.loop(0, INNER)
    def _(c):
        out[c] = right_product(work[c], table)


def move_rows(sense, data, factor, forward, backward, twist, out, work, spectrum):
    @pl.loop(0, RADIX // 8)
    def _(i):
        here = row_chunk(i)
        below = pl.ds(pl.multiple_of(RADIX + i * 8, 8), 8)
        values = [(data[a, here, :RADIX], data[a, here, RADIX:]) for a in range(INNER)]
        for c, (re, im) in enumerate(butterflies(values, -1.0)):
            tr, ti = twist[0, c, here, :], twist[1, c, here, :]
            side = slice((c % 2) * RADIX, (c % 2 + 1) * RADIX)
            work[c // 2, here, side] = re * tr - im * ti
            work[c // 2, below, side] = re * ti + im * tr

    @pl.loop(0, INNER // 2)
    def _(p):
        spectrum[p] = left_product(forward, work[p])

    for which in range(NREF):

        @pl.loop(0, INNER // 2)
        def _(p):
            re, im = spectrum[p, :RADIX, :], spectrum[p, RADIX:, :]
            fr, fi = factor[which, 0, p], sense * factor[which, 1, p]
            moved = jnp.concatenate([re * fr - im * fi, re * fi + im * fr], axis=0)
            work[p] = left_product(backward, moved)

        @pl.loop(0, RADIX // 8)
        def _(i):
            here = row_chunk(i)
            below = pl.ds(pl.multiple_of(RADIX + i * 8, 8), 8)
            values = []
            for c in range(INNER):
                side = slice((c % 2) * RADIX, (c % 2 + 1) * RADIX)
                re, im = work[c // 2, here, side], work[c // 2, below, side]
                tr, ti = twist[0, c, here, :], twist[1, c, here, :]
                values.append((re * tr + im * ti, im * tr - re * ti))
            for a, (re, im) in enumerate(butterflies(values, 1.0)):
                out[a, which, here, :RADIX] = re
                out[a, which, here, RADIX:] = im


def backward_columns(data, chosen, table, twist, *rest):
    other, out, work, keep = rest if len(rest) == 4 else (None, *rest)
    rows = data.shape[2]
    for which in range(NREF):
        flat = data[:, which].reshape(INNER * rows, 2 * RADIX)
        work[...] = right_product(flat, table).reshape(INNER, rows, 2 * RADIX)

        @pl.loop(0, rows // 8)
        def _(i):
            here = row_chunk(i)
            values = []
            for c in range(INNER):
                re, im = work[c, here, :RADIX], work[c, here, RADIX:]
                tr, ti = twist[0, c : c + 1, :], twist[1, c : c + 1, :]
                values.append((re * tr + im * ti, im * tr - re * ti))
            for a, (re, im) in enumerate(butterflies(values, 1.0)):
                side = slice(a * RADIX, (a + 1) * RADIX)
                if which > 0:
                    mine = chosen[here, side] == which
                    re = jnp.where(mine, re, keep[0, here, side])
                    im = jnp.where(mine, im, keep[1, here, side])
                if which < NREF - 1:
                    keep[0, here, side] = re
                    keep[1, here, side] = im
                elif other is None:
                    out[0, here, side] = re
                    out[1, here, side] = im
                else:
                    out[here, side] = other[0, here, side] * re + other[1, here, side] * im


def f32(*shape):
    return jax.ShapeDtypeStruct(shape, jnp.float32)


def cost(us_bytes):
    return pl.CostEstimate(flops=2 * 10**9, bytes_accessed=us_bytes, transcendentals=0)


def series(square, start):
    total = jnp.full_like(square, (-1.0) ** 10 / math.factorial(20 + start))
    for k in range(9, -1, -1):
        total = total * square + (-1.0) ** k / math.factorial(2 * k + start)
    return total


def per_device(
    source_field, rec_blocks, dest_device, dest_bin, slowness, ref_index, ref_slow, omega
):
    lanes = lax.axis_size("lat")
    rows = source_field.shape[2]
    columns = source_field.shape[3]
    width = rec_blocks.shape[3]
    fits = lanes == INNER and rows == RADIX and columns == LENGTH and width == RADIX
    if not fits or rec_blocks.shape[2] != 1 or source_field.shape[1] != 1:
        return general(
            source_field, rec_blocks, dest_device, dest_bin, slowness, ref_index, ref_slow, omega
        )
    me = lax.axis_index("lat")
    count = rec_blocks.shape[0]
    per_row = columns // width
    right_forward, right_backward = dft_tables(-1.0, False, 1.0), dft_tables(1.0, False, 1.0 / LENGTH)
    left_forward, left_backward = dft_tables(-1.0, True, 1.0), dft_tables(1.0, True, 1.0 / LENGTH)
    twist = jnp.asarray(twiddles(-1.0))
    wide_twist = jnp.broadcast_to(twist[:, :, :, None], (2, INNER, RADIX, RADIX))
    target = dest_device[:, 0] * (rows * per_row) + dest_bin
    packed = jnp.concatenate(
        [
            rec_blocks.reshape(count, 2 * width),
            jnp.broadcast_to(target.astype(jnp.float32)[:, None], (count, width)),
        ],
        axis=1,
    )
    copies = jnp.broadcast_to(packed[None], (lanes,) + packed.shape)
    packed = lax.all_to_all(copies, "lat", split_axis=0, concat_axis=0, tiled=True)

    spectrum = pl.pallas_call(
        forward_columns,
        out_shape=f32(INNER, rows, 2 * RADIX),
        scratch_shapes=[pltpu.VMEM((INNER, rows, 2 * RADIX), jnp.float32)],
        compiler_params=PARAMS,
        cost_estimate=cost(2**23),
        name="forward_columns",
    )(source_field[:, 0], right_forward, twist)
    packed, spectrum = lax.optimization_barrier((packed, spectrum))
    packed = packed.reshape(lanes * count, 3 * width)
    source_part = lax.all_to_all(spectrum, "lat", split_axis=0, concat_axis=0, tiled=True)

    step = 2.0 * math.pi / (LENGTH * SPACING) * DEPTH_STEP
    number = jnp.arange(LENGTH, dtype=jnp.int32)
    signed = jnp.where(number < LENGTH // 2, number, number - LENGTH).astype(jnp.float32) * step
    squares = (signed * signed).reshape(RADIX, INNER)
    kx_square = squares.T.reshape(INNER // 2, 2, RADIX).transpose(0, 2, 1)
    ky_square = lax.dynamic_slice_in_dim(squares, me, 1, axis=1)[:, 0]
    radial = (kx_square[:, :, :, None] + ky_square).reshape(INNER // 2, RADIX, 2 * RADIX)
    limit = (omega[0] * ref_slow[0] * DEPTH_STEP) ** 2
    argument = limit[:, None, None, None] - radial[None]
    inside = jnp.maximum(argument, 0.0)
    amplitude = jnp.exp(-jnp.sqrt(jnp.maximum(-argument, 0.0)))
    factor = jnp.stack(
        [
            amplitude * series(inside, 0),
            jnp.sign(omega[0]) * amplitude * jnp.sqrt(inside) * series(inside, 1),
        ],
        axis=1,
    )

    def propagate(part, sense, label):
        return pl.pallas_call(
            partial(move_rows, sense),
            out_shape=f32(INNER, NREF, RADIX, 2 * RADIX),
            scratch_shapes=[
                pltpu.VMEM((INNER // 2, 2 * RADIX, 2 * RADIX), jnp.float32),
                pltpu.VMEM((INNER // 2, 2 * RADIX, 2 * RADIX), jnp.float32),
            ],
            compiler_params=PARAMS,
            cost_estimate=cost(2**25),
            name="move_rows_" + label,
        )(part, factor, left_forward, left_backward, wide_twist)

    def send_back(moved):
        return lax.all_to_all(moved, "lat", split_axis=0, concat_axis=0, tiled=True)


    target = jnp.round(packed[:, 2 * width]).astype(jnp.int32)
    row, place = target // per_row, target % per_row
    own = lax.dynamic_slice_in_dim(twist, me, 1, axis=1)[:, 0]
    turn = (place * me % INNER).astype(jnp.float32) * (-2.0 * math.pi / INNER)
    turn_real, turn_imag = jnp.cos(turn)[:, None], jnp.sin(turn)[:, None]
    weight_real = turn_real * own[0] - turn_imag * own[1]
    weight_imag = turn_real * own[1] + turn_imag * own[0]
    real, imag = packed[:, :width], packed[:, width : 2 * width]
    turned = jnp.concatenate(
        [real * weight_real - imag * weight_imag, real * weight_imag + imag * weight_real], axis=1
    )
    whole_table = right_forward[0].astype(jnp.float32) + right_forward[1].astype(jnp.float32)
    traces = jnp.dot(turned, whole_table, precision=lax.Precision.HIGHEST)
    spread = (jnp.arange(lanes * rows, dtype=jnp.int32)[:, None] == row[None, :]).astype(jnp.float32)
    received_part = jnp.dot(spread, traces, precision=lax.Precision.HIGHEST)
    received_part = received_part.reshape(INNER, RADIX, 2 * RADIX)

    chosen = ref_index[0]

    share = rows // 4

    def restore(back, label, *other):
        fields = pl.BlockSpec((2, share, columns), lambda i: (0, i, 0))
        plane = pl.BlockSpec((share, columns), lambda i: (i, 0))
        return pl.pallas_call(
            backward_columns,
            grid=(rows // share,),
            in_specs=[
                pl.BlockSpec((INNER, NREF, share, 2 * RADIX), lambda i: (0, 0, i, 0)),
                plane,
                pl.BlockSpec((2, 2 * RADIX, 2 * RADIX), lambda i: (0, 0, 0)),
                pl.BlockSpec((2, INNER, RADIX), lambda i: (0, 0, 0)),
            ]
            + [fields] * len(other),
            out_specs=plane if other else fields,
            out_shape=f32(rows, columns) if other else f32(2, rows, columns),
            scratch_shapes=[
                pltpu.VMEM((INNER, share, 2 * RADIX), jnp.float32),
                pltpu.VMEM((2, share, columns), jnp.float32),
            ],
            compiler_params=PARAMS,
            cost_estimate=cost(2**24),
            name="backward_columns_" + label,
        )(back, chosen, right_backward, twist, *other)

    moved = propagate(received_part, 1.0, "received")
    moved, source_part = lax.optimization_barrier((moved, source_part))
    received_back = send_back(moved)
    moved = propagate(source_part, -1.0, "source")
    moved, received_back = lax.optimization_barrier((moved, received_back))
    source_back = send_back(moved)
    received = restore(received_back, "received")
    speed = jnp.where(chosen == 1, ref_slow[0, 1], ref_slow[0, 0])
    double = (2.0 * DEPTH_STEP) * omega[0] * (slowness[0] - speed)
    square = double * double
    cosine, sine = series(square, 0), double * series(square, 1)
    turned = jnp.stack(
        [received[0] * cosine - received[1] * sine, received[1] * cosine + received[0] * sine]
    )
    return restore(source_back, "image", turned)[None]


def solution(mesh):
    return jax.shard_map(
        per_device,
        mesh=mesh,
        in_specs=(
            P(None, "shots", "lat", None),
            P(("shots", "lat"), None, None, None),
            P(("shots", "lat"), None),
            P(("shots", "lat")),
            P(None, "lat", None),
            P(None, "lat", None),
            P(),
            P(),
        ),
        out_specs=P("shots", "lat", None),
        check_vma=False,
    )
```

```python
from functools import partial
import math

import jax
import jax.numpy as jnp
import numpy as np
from jax import lax
from jax.experimental import pallas as pl
from jax.experimental.pallas import tpu as pltpu
from jax.sharding import PartitionSpec as P

NREF = 2
CAP = 2


SPACING = 0.01
DEPTH_STEP = 0.01
RADIX = 128


def angle_table(size, direction):
    index = jnp.arange(size, dtype=jnp.int32)
    product = index[:, None] * index[None, :] % size
    angle = direction * 2.0 * math.pi * product.astype(jnp.float32) / size
    return (jnp.cos(angle), jnp.sin(angle))


def twist_table(length, direction):
    outer_index = jnp.arange(length // RADIX, dtype=jnp.int32)
    radix_index = jnp.arange(RADIX, dtype=jnp.int32)
    product = outer_index[:, None] * radix_index[None, :] % length
    angle = direction * 2.0 * math.pi * product.astype(jnp.float32) / length
    return (jnp.cos(angle), jnp.sin(angle))


def complex_einsum(formula, real_in, imag_in, real_mat, imag_mat):
    multiply = partial(jnp.einsum, formula, precision=lax.Precision.HIGHEST)
    return (
        multiply(real_in, real_mat) - multiply(imag_in, imag_mat),
        multiply(real_in, imag_mat) + multiply(imag_in, real_mat),
    )


def transform(real_in, imag_in, trailing, direction):
    length = real_in.shape[-2] if trailing else real_in.shape[-1]
    inner = length // RADIX
    first_real, first_imag = angle_table(inner, direction)
    second_real, second_imag = angle_table(RADIX, direction)
    twist_real, twist_imag = twist_table(length, direction)
    initial = real_in.shape
    if trailing:
        shape = initial[:-2] + (inner, RADIX, initial[-1])
        twist_real = twist_real[:, :, None]
        twist_imag = twist_imag[:, :, None]
        tail = "z"
    else:
        shape = initial[:-1] + (inner, RADIX)
        tail = ""
    work_real = real_in.reshape(shape)
    work_imag = imag_in.reshape(shape)
    if direction < 0:
        work_real, work_imag = complex_einsum(
            "...ab" + tail + ",ac->...cb" + tail, work_real, work_imag, first_real, first_imag
        )
        work_real, work_imag = (
            work_real * twist_real - work_imag * twist_imag,
            work_real * twist_imag + work_imag * twist_real,
        )
        work_real, work_imag = complex_einsum(
            "...cb" + tail + ",bd->...cd" + tail, work_real, work_imag, second_real, second_imag
        )
    else:
        work_real, work_imag = complex_einsum(
            "...cb" + tail + ",bd->...cd" + tail, work_real, work_imag, second_real, second_imag
        )
        work_real, work_imag = (
            work_real * twist_real - work_imag * twist_imag,
            work_real * twist_imag + work_imag * twist_real,
        )
        work_real, work_imag = complex_einsum(
            "...cb" + tail + ",ca->...ab" + tail, work_real, work_imag, first_real, first_imag
        )
        work_real = work_real / length
        work_imag = work_imag / length
    return (work_real.reshape(initial), work_imag.reshape(initial))


def permuted_numbers(positions, length):
    inner = length // RADIX
    index = positions // RADIX + inner * (positions % RADIX)
    signed = jnp.where(index < length // 2, index, index - length)
    return signed.astype(jnp.float32) * (2.0 * math.pi / (length * SPACING))


def general(
    source_field, rec_blocks, dest_device, dest_bin, slowness, ref_index, ref_slow, omega
):
    lanes = lax.axis_size("lat")
    count_blocks = rec_blocks.shape[0]
    freqs = rec_blocks.shape[2]
    block_width = rec_blocks.shape[3]
    rows_here = source_field.shape[2]
    columns = source_field.shape[3]
    bins_here = rows_here * (columns // block_width)
    slots = lanes * CAP
    flat = rec_blocks.reshape(count_blocks, 2 * freqs * block_width)
    onehot = (dest_device == jnp.arange(lanes, dtype=jnp.int32)[None, :]).astype(jnp.int32)
    order = jnp.arange(count_blocks, dtype=jnp.int32)
    before = (order[None, :] < order[:, None]).astype(jnp.int32)
    earlier = jnp.sum(before[:, :, None] * onehot[None, :, :], axis=1)
    ranking = jnp.sum(onehot * earlier, axis=1)
    slot_of = dest_device[:, 0] * CAP + ranking
    placing = slot_of[None, :] == jnp.arange(slots, dtype=jnp.int32)[:, None]
    outgoing = jnp.dot(placing.astype(jnp.float32), flat, precision=lax.Precision.HIGHEST)
    labels = jnp.sum(jnp.where(placing, (dest_bin + 1)[None, :], 0), axis=1).astype(jnp.float32)
    arrived, arrived_labels = (
        lax.all_to_all(
            outgoing.reshape(lanes, CAP, -1), "lat", split_axis=0, concat_axis=0, tiled=True
        ),
        lax.all_to_all(labels.reshape(lanes, CAP), "lat", split_axis=0, concat_axis=0, tiled=True),
    )
    bin_labels = arrived_labels.reshape(slots).astype(jnp.int32) - 1
    gathering = (bin_labels[None, :] == jnp.arange(bins_here, dtype=jnp.int32)[:, None]).astype(
        jnp.float32
    )
    binned = jnp.dot(gathering, arrived.reshape(slots, -1), precision=lax.Precision.HIGHEST)
    binned = binned.reshape(rows_here, columns // block_width, 2, freqs, block_width)
    received = binned.transpose(2, 3, 0, 1, 4).reshape(2, freqs, rows_here, columns)
    field_real = jnp.concatenate([source_field[0], received[0]], axis=0)
    field_imag = jnp.concatenate([source_field[1], received[1]], axis=0)
    signed = jnp.concatenate([-omega, omega])
    spec_real, spec_imag = transform(field_real, field_imag, False, -1.0)
    carried = jnp.broadcast_to(signed[:, None, None], (2 * freqs, 1, lanes))
    part_real = lax.all_to_all(spec_real, "lat", split_axis=2, concat_axis=1, tiled=True)
    part_imag = lax.all_to_all(spec_imag, "lat", split_axis=2, concat_axis=1, tiled=True)
    part_params = lax.all_to_all(carried, "lat", split_axis=2, concat_axis=1, tiled=True)
    total_rows = part_real.shape[1]
    local_cols = part_real.shape[2]
    freq_real, freq_imag = transform(part_real, part_imag, True, -1.0)
    kx_values = permuted_numbers(jnp.arange(total_rows, dtype=jnp.int32), total_rows)
    positions = lax.axis_index("lat") * local_cols + jnp.arange(local_cols, dtype=jnp.int32)
    ky_values = permuted_numbers(positions, lanes * local_cols)
    radial = kx_values[:, None] ** 2 + ky_values[None, :] ** 2
    freq_signed = part_params[:, 0, 0]
    sense = jnp.sign(freq_signed)[:, None, None]
    shifted_real = []
    shifted_imag = []
    for propagate_which in range(NREF):
        propagate_speed = ref_slow[0, propagate_which]
        argument = (freq_signed**2)[:, None, None] * propagate_speed**2 - radial[None]
        amplitude = jnp.exp(-jnp.sqrt(jnp.maximum(-argument, 0.0)) * DEPTH_STEP)
        phase = sense * jnp.sqrt(jnp.maximum(argument, 0.0)) * DEPTH_STEP
        factor_real = amplitude * jnp.cos(phase)
        factor_imag = amplitude * jnp.sin(phase)
        moved_real = freq_real * factor_real - freq_imag * factor_imag
        moved_imag = freq_real * factor_imag + freq_imag * factor_real
        moved_real, moved_imag = transform(moved_real, moved_imag, True, 1.0)
        shifted_real.append(moved_real)
        shifted_imag.append(moved_imag)
    stacked_real = jnp.stack(shifted_real, axis=1)
    stacked_imag = jnp.stack(shifted_imag, axis=1)
    back_real = lax.all_to_all(stacked_real, "lat", split_axis=2, concat_axis=3, tiled=True)
    back_imag = lax.all_to_all(stacked_imag, "lat", split_axis=2, concat_axis=3, tiled=True)
    space_real, space_imag = transform(back_real, back_imag, False, 1.0)
    new_real = jnp.zeros_like(field_real)
    new_imag = jnp.zeros_like(field_imag)
    for which in range(NREF):
        speed = ref_slow[0, which]
        angle = signed[:, None, None] * (slowness[0] - speed)[None] * DEPTH_STEP
        cosine = jnp.cos(angle)
        sine = jnp.sin(angle)
        fixed_real = space_real[:, which] * cosine - space_imag[:, which] * sine
        fixed_imag = space_real[:, which] * sine + space_imag[:, which] * cosine
        chosen = (ref_index[0] == which)[None]
        new_real = jnp.where(chosen, fixed_real, new_real)
        new_imag = jnp.where(chosen, fixed_imag, new_imag)
    images = [
        jnp.sum(new_real[:freqs] * new_real[freqs:] + new_imag[:freqs] * new_imag[freqs:], axis=0)
    ]
    return jnp.stack(images)


INNER = 16
LENGTH = INNER * RADIX
PARAMS = pltpu.CompilerParams(vmem_limit_bytes=50 * 2**20)


def dft_tables(direction, left, scale):
    index = np.arange(RADIX)
    angle = direction * 2.0 * np.pi * (index[:, None] * index[None, :] % RADIX) / RADIX
    cosine, sine = np.cos(angle) * scale, np.sin(angle) * scale
    whole = np.block([[cosine, -sine], [sine, cosine]] if left else [[cosine, sine], [-sine, cosine]])
    whole = jnp.asarray(whole.astype(np.float32))
    high = whole.astype(jnp.bfloat16)
    low = (whole - high.astype(jnp.float32)).astype(jnp.bfloat16)
    return jnp.stack([high, low])


def twiddles(direction):
    angle = direction * 2.0 * np.pi * (np.arange(INNER)[:, None] * np.arange(RADIX)[None, :]) / LENGTH
    return np.stack([np.cos(angle), np.sin(angle)]).astype(np.float32)


def butterflies(values, direction):
    count = len(values)
    if count == 1:
        return values
    even = butterflies(values[0::2], direction)
    odd = butterflies(values[1::2], direction)
    first, second = [], []
    for k in range(count // 2):
        (er, ei), (pr, pi) = even[k], odd[k]
        if k == 0:
            tr, ti = pr, pi
        elif 4 * k == count:
            tr, ti = (-pi, pr) if direction > 0 else (pi, -pr)
        else:
            c = math.cos(2.0 * math.pi * k / count)
            d = direction * math.sin(2.0 * math.pi * k / count)
            tr, ti = pr * c - pi * d, pr * d + pi * c
        first.append((er + tr, ei + ti))
        second.append((er - tr, ei - ti))
    return first + second


def halves(value):
    high = value.astype(jnp.bfloat16)
    return high, (value - high.astype(jnp.float32)).astype(jnp.bfloat16)


def mul(a, b):
    return jnp.dot(a, b, preferred_element_type=jnp.float32)


def right_product(value, table):
    high, low = halves(value)
    return mul(low, table[0]) + mul(high, table[1]) + mul(high, table[0])


def left_product(table, value):
    high, low = halves(value)
    return mul(table[1], high) + mul(table[0], low) + mul(table[0], high)


def row_chunk(i):
    return pl.ds(pl.multiple_of(i * 8, 8), 8)


def forward_columns(field, table, twist, out, work):
    rows = field.shape[1]

    @pl.loop(0, rows // 8)
    def _(i):
        here = row_chunk(i)
        values = [
            (
                field[0, here, a * RADIX : (a + 1) * RADIX],
                field[1, here, a * RADIX : (a + 1) * RADIX],
            )
            for a in range(INNER)
        ]
        for c, (re, im) in enumerate(butterflies(values, -1.0)):
            tr, ti = twist[0, c : c + 1, :], twist[1, c : c + 1, :]
            work[c, here, :RADIX] = re * tr - im * ti
            work[c, here, RADIX:] = re * ti + im * tr

    @pl.loop(0, INNER)
    def _(c):
        out[c] = right_product(work[c], table)


def move_rows(sense, data, factor, forward, backward, twist, out, work, spectrum):
    @pl.loop(0, RADIX // 8)
    def _(i):
        here = row_chunk(i)
        below = pl.ds(pl.multiple_of(RADIX + i * 8, 8), 8)
        values = [(data[a, here, :RADIX], data[a, here, RADIX:]) for a in range(INNER)]
        for c, (re, im) in enumerate(butterflies(values, -1.0)):
            tr, ti = twist[0, c, here, :], twist[1, c, here, :]
            side = slice((c % 2) * RADIX, (c % 2 + 1) * RADIX)
            work[c // 2, here, side] = re * tr - im * ti
            work[c // 2, below, side] = re * ti + im * tr

    @pl.loop(0, INNER // 2)
    def _(p):
        spectrum[p] = left_product(forward, work[p])

    for which in range(NREF):

        @pl.loop(0, INNER // 2)
        def _(p):
            re, im = spectrum[p, :RADIX, :], spectrum[p, RADIX:, :]
            fr, fi = factor[which, 0, p], sense * factor[which, 1, p]
            moved = jnp.concatenate([re * fr - im * fi, re * fi + im * fr], axis=0)
            work[p] = left_product(backward, moved)

        @pl.loop(0, RADIX // 8)
        def _(i):
            here = row_chunk(i)
            below = pl.ds(pl.multiple_of(RADIX + i * 8, 8), 8)
            values = []
            for c in range(INNER):
                side = slice((c % 2) * RADIX, (c % 2 + 1) * RADIX)
                re, im = work[c // 2, here, side], work[c // 2, below, side]
                tr, ti = twist[0, c, here, :], twist[1, c, here, :]
                values.append((re * tr + im * ti, im * tr - re * ti))
            for a, (re, im) in enumerate(butterflies(values, 1.0)):
                out[a, which, here, :RADIX] = re
                out[a, which, here, RADIX:] = im


def backward_columns(data, chosen, table, twist, *rest):
    other, out, work, keep = rest if len(rest) == 4 else (None, *rest)
    rows = data.shape[2]
    for which in range(NREF):
        flat = data[:, which].reshape(INNER * rows, 2 * RADIX)
        work[which] = right_product(flat, table).reshape(INNER, rows, 2 * RADIX)

        @pl.loop(0, rows // 8, unroll=True)
        def _(i):
            here = row_chunk(i)
            values = []
            for c in range(INNER):
                re, im = work[which, c, here, :RADIX], work[which, c, here, RADIX:]
                tr, ti = twist[0, c : c + 1, :], twist[1, c : c + 1, :]
                values.append((re * tr + im * ti, im * tr - re * ti))
            for a, (re, im) in enumerate(butterflies(values, 1.0)):
                side = slice(a * RADIX, (a + 1) * RADIX)
                if which > 0:
                    mine = chosen[here, side] == which
                    re = jnp.where(mine, re, keep[0, here, side])
                    im = jnp.where(mine, im, keep[1, here, side])
                if which < NREF - 1:
                    keep[0, here, side] = re
                    keep[1, here, side] = im
                elif other is None:
                    out[0, here, side] = re
                    out[1, here, side] = im
                else:
                    out[here, side] = other[0, here, side] * re + other[1, here, side] * im


def f32(*shape):
    return jax.ShapeDtypeStruct(shape, jnp.float32)


def cost(us_bytes):
    return pl.CostEstimate(flops=2 * 10**9, bytes_accessed=us_bytes, transcendentals=0)


def series(square, start):
    total = jnp.full_like(square, (-1.0) ** 10 / math.factorial(20 + start))
    for k in range(9, -1, -1):
        total = total * square + (-1.0) ** k / math.factorial(2 * k + start)
    return total


def per_device(
    source_field, rec_blocks, dest_device, dest_bin, slowness, ref_index, ref_slow, omega
):
    lanes = lax.axis_size("lat")
    rows = source_field.shape[2]
    columns = source_field.shape[3]
    width = rec_blocks.shape[3]
    fits = lanes == INNER and rows == RADIX and columns == LENGTH and width == RADIX
    fits = fits and rec_blocks.shape[0] <= RADIX
    if not fits or rec_blocks.shape[2] != 1 or source_field.shape[1] != 1:
        return general(
            source_field, rec_blocks, dest_device, dest_bin, slowness, ref_index, ref_slow, omega
        )
    me = lax.axis_index("lat")
    count = rec_blocks.shape[0]
    per_row = columns // width
    right_forward, right_backward = dft_tables(-1.0, False, 1.0), dft_tables(1.0, False, 1.0 / LENGTH)
    left_forward, left_backward = dft_tables(-1.0, True, 1.0), dft_tables(1.0, True, 1.0 / LENGTH)
    twist = jnp.asarray(twiddles(-1.0))
    wide_twist = jnp.broadcast_to(twist[:, :, :, None], (2, INNER, RADIX, RADIX))
    target = dest_device[:, 0] * (rows * per_row) + dest_bin
    packed = jnp.concatenate(
        [
            rec_blocks.reshape(2 * count, width),
            jnp.pad(target.astype(jnp.float32), (0, width - count))[None],
        ],
        axis=0,
    )
    copies = jnp.broadcast_to(packed[None], (lanes,) + packed.shape)
    packed = lax.all_to_all(copies, "lat", split_axis=0, concat_axis=0, tiled=True)

    spectrum = pl.pallas_call(
        forward_columns,
        out_shape=f32(INNER, rows, 2 * RADIX),
        scratch_shapes=[pltpu.VMEM((INNER, rows, 2 * RADIX), jnp.float32)],
        compiler_params=PARAMS,
        cost_estimate=cost(2**23),
        name="forward_columns",
    )(source_field[:, 0], right_forward, twist)
    packed, spectrum = lax.optimization_barrier((packed, spectrum))
    blocks = packed[:, : 2 * count].reshape(lanes * count, 2 * width)
    source_part = lax.all_to_all(spectrum, "lat", split_axis=0, concat_axis=0, tiled=True)

    step = 2.0 * math.pi / (LENGTH * SPACING) * DEPTH_STEP
    number = jnp.arange(LENGTH, dtype=jnp.int32)
    signed = jnp.where(number < LENGTH // 2, number, number - LENGTH).astype(jnp.float32) * step
    squares = (signed * signed).reshape(RADIX, INNER)
    kx_square = squares.T.reshape(INNER // 2, 2, RADIX).transpose(0, 2, 1)
    ky_square = lax.dynamic_slice_in_dim(squares, me, 1, axis=1)[:, 0]
    radial = (kx_square[:, :, :, None] + ky_square).reshape(INNER // 2, RADIX, 2 * RADIX)
    limit = (omega[0] * ref_slow[0] * DEPTH_STEP) ** 2
    argument = limit[:, None, None, None] - radial[None]
    inside = jnp.maximum(argument, 0.0)
    amplitude = jnp.exp(-jnp.sqrt(jnp.maximum(-argument, 0.0)))
    factor = jnp.stack(
        [
            amplitude * series(inside, 0),
            jnp.sign(omega[0]) * amplitude * jnp.sqrt(inside) * series(inside, 1),
        ],
        axis=1,
    )

    def propagate(part, sense, label):
        return pl.pallas_call(
            partial(move_rows, sense),
            out_shape=f32(INNER, NREF, RADIX, 2 * RADIX),
            scratch_shapes=[
                pltpu.VMEM((INNER // 2, 2 * RADIX, 2 * RADIX), jnp.float32),
                pltpu.VMEM((INNER // 2, 2 * RADIX, 2 * RADIX), jnp.float32),
            ],
            compiler_params=PARAMS,
            cost_estimate=cost(2**25),
            name="move_rows_" + label,
        )(part, factor, left_forward, left_backward, wide_twist)

    def send_back(moved):
        return lax.all_to_all(moved, "lat", split_axis=0, concat_axis=0, tiled=True)


    target = jnp.round(packed[:, 2 * count, :count].reshape(-1)).astype(jnp.int32)
    row, place = target // per_row, target % per_row
    own = lax.dynamic_slice_in_dim(twist, me, 1, axis=1)[:, 0]
    turn = (place * me % INNER).astype(jnp.float32) * (-2.0 * math.pi / INNER)
    turn_real, turn_imag = jnp.cos(turn)[:, None], jnp.sin(turn)[:, None]
    weight_real = turn_real * own[0] - turn_imag * own[1]
    weight_imag = turn_real * own[1] + turn_imag * own[0]
    real, imag = blocks[:, :width], blocks[:, width:]
    turned = jnp.concatenate(
        [real * weight_real - imag * weight_imag, real * weight_imag + imag * weight_real], axis=1
    )
    whole_table = right_forward[0].astype(jnp.float32) + right_forward[1].astype(jnp.float32)
    traces = jnp.dot(turned, whole_table, precision=lax.Precision.HIGHEST)
    spread = (jnp.arange(lanes * rows, dtype=jnp.int32)[:, None] == row[None, :]).astype(jnp.float32)
    received_part = jnp.dot(spread, traces, precision=lax.Precision.HIGHEST)
    received_part = received_part.reshape(INNER, RADIX, 2 * RADIX)

    chosen = ref_index[0]

    share = rows // 4

    def restore(back, label, *other):
        fields = pl.BlockSpec((2, share, columns), lambda i: (0, i, 0))
        plane = pl.BlockSpec((share, columns), lambda i: (i, 0))
        return pl.pallas_call(
            backward_columns,
            grid=(rows // share,),
            in_specs=[
                pl.BlockSpec((INNER, NREF, share, 2 * RADIX), lambda i: (0, 0, i, 0)),
                plane,
                pl.BlockSpec((2, 2 * RADIX, 2 * RADIX), lambda i: (0, 0, 0)),
                pl.BlockSpec((2, INNER, RADIX), lambda i: (0, 0, 0)),
            ]
            + [fields] * len(other),
            out_specs=plane if other else fields,
            out_shape=f32(rows, columns) if other else f32(2, rows, columns),
            scratch_shapes=[
                pltpu.VMEM((NREF, INNER, share, 2 * RADIX), jnp.float32),
                pltpu.VMEM((2, share, columns), jnp.float32),
            ],
            compiler_params=PARAMS,
            cost_estimate=cost(2**24),
            name="backward_columns_" + label,
        )(back, chosen, right_backward, twist, *other)

    moved = propagate(received_part, 1.0, "received")
    moved, source_part = lax.optimization_barrier((moved, source_part))
    received_back = send_back(moved)
    moved = propagate(source_part, -1.0, "source")
    moved, received_back = lax.optimization_barrier((moved, received_back))
    source_back = send_back(moved)
    received = restore(received_back, "received")
    speed = jnp.where(chosen == 1, ref_slow[0, 1], ref_slow[0, 0])
    double = (2.0 * DEPTH_STEP) * omega[0] * (slowness[0] - speed)
    square = double * double
    cosine, sine = series(square, 0), double * series(square, 1)
    turned = jnp.stack(
        [received[0] * cosine - received[1] * sine, received[1] * cosine + received[0] * sine]
    )
    return restore(source_back, "image", turned)[None]


def solution(mesh):
    return jax.shard_map(
        per_device,
        mesh=mesh,
        in_specs=(
            P(None, "shots", "lat", None),
            P(("shots", "lat"), None, None, None),
            P(("shots", "lat"), None),
            P(("shots", "lat")),
            P(None, "lat", None),
            P(None, "lat", None),
            P(),
            P(),
        ),
        out_specs=P("shots", "lat", None),
        check_vma=False,
    )
```
